32 devices in a mesh: survey: 2 (over x), sub: 8 (over z, y), freq: 2 (over core).
Axes of the slice: x: 2, y: 2, z: 4, core: 2. Of those that a mesh axis runs over, the one named last changes fastest.
Arguments:
- trace_map: bfloat16 [4, 32, 2, 768, 768], P('freq', ('survey', 'sub')), parts along dimension 1, may hold values from -0.109375 to 0.109375
- interior_map: bfloat16 [4, 32, 2, 768, 768], P('freq', ('survey', 'sub')), parts along dimension 1, may hold values from -0.15625 to 0.15625
- excitation: bfloat16 [4, 32, 768, 2, 128], P('freq', ('survey', 'sub')), parts along dimension 1, may hold values from -6 to 6
- receiver_data: bfloat16 [4, 32, 768, 2, 128], P('freq', ('survey', 'sub')), parts along dimension 1, may hold values from -6 to 6
- shot_index: int32 [128], P('survey'), parts along dimension 0, may hold values from 0 to 127, as said below
Outputs:
- image: float32 [32, 768, 768], P(('survey', 'sub'), 'freq'), parts along dimension 0
The draws below stay inside these ranges and needn't reach their ends.
There are 2 independent parts, one for each index of `survey`. The reference program is written for one: setup_inputs(seed, part) draws one part's arguments, and reference() takes and returns one part's arrays. A program takes and returns all parts, laid end to end along the dimension named above; each array names one. Nothing has to cross between parts.
Inputs may be any that keep to these rules, and one draw needn't show every extreme that they name: `shot_index`: 64 distinct shot numbers in shuffled order; 0 and 127 are always among them.
All inputs are finite; a program needn't handle non-finite values.
Results may differ from the reference program's by a relative error of at most 0.0094.
Values may be sent and summed in bfloat16 or wider, within the bound.
No kernel may reach another device: no remote copies, remote signals or barrier semaphores. Data moves between devices by JAX's collectives and lax.ppermute only.
A program may use at most 128 MiB of HBM per device.

```python
import jax
import jax.numpy as jnp

K = 768
GY = 4
TICKS = 6
BANK = 128
NS = 64
S = 16
GX = 4
FREQS = 4


def draw_shot_index(key, part):
    first_key = jax.random.fold_in(key, 11)
    second_key = jax.random.fold_in(key, 23)
    middle = 1 + jax.random.permutation(first_key, BANK - 2)[:NS - 2]
    chosen = jnp.concatenate([jnp.array([0, BANK - 1], jnp.int32), middle.astype(jnp.int32)])
    order = jax.random.permutation(second_key, NS)
    return chosen[order].astype(jnp.int32)


def block_scale(stream_key, shape, pieces, least, top_value):
    gain = 1.0
    for position, blocks in pieces:
        steps = jax.random.uniform(jax.random.fold_in(jax.random.fold_in(stream_key, 6), position), (blocks,), jnp.float32, least / len(pieces), top_value / len(pieces))
        gain = gain * jnp.repeat(jnp.exp(steps), shape[position] // blocks).reshape((-1,) + (1,) * (len(shape) - 1 - position))
    return gain


def bell_draw(own_key, dims, scale, limit, split=(), kind=jnp.bfloat16):
    loudness = block_scale(own_key, dims, split, -0.22, 0.18) if split else 1.0
    entries = jax.random.normal(own_key, dims, jnp.float32) * scale * loudness
    return jnp.minimum(jnp.maximum(entries, -limit), limit).astype(kind)


def setup_inputs(seed: int = 0, part: int = 0) -> dict:
    splits = jax.random.split(jax.random.key(seed), 6)
    part_splits = jax.random.split(jax.random.fold_in(splits[5], part), 6)
    return {
        "trace_map": bell_draw(part_splits[0], (FREQS, S, 2, K, K), (4 * K) ** -0.5, 0.109375, ((0, 2), (1, 8))),
        "interior_map": bell_draw(part_splits[1], (FREQS, S, 2, K, K), (2 * K) ** -0.5, 0.15625, ((0, 2), (1, 8))),
        "excitation": bell_draw(part_splits[2], (FREQS, S, K, 2, BANK), 1.0, 6.0, ((0, 2), (1, 8))),
        "receiver_data": bell_draw(part_splits[3], (FREQS, S, K, 2, BANK), 1.0, 6.0, ((0, 2), (1, 8))),
        "shot_index": draw_shot_index(jax.random.fold_in(jax.random.fold_in(splits[5], part), 71), part),
    }


def forward_apply(maps, front):
    values = front.astype(jnp.float32)
    product = jnp.einsum("fsckm,fsmn->fsckn", maps, values)
    real_part = product[:, :, 0, :, :NS] - product[:, :, 1, :, NS:]
    imag_part = product[:, :, 0, :, NS:] + product[:, :, 1, :, :NS]
    return jnp.concatenate([real_part, imag_part], axis=-1)


def adjoint_apply(maps, front):
    values = front.astype(jnp.float32)
    product = jnp.einsum("fsckm,fskn->fscmn", maps, values)
    real_part = product[:, :, 0, :, :NS] + product[:, :, 1, :, NS:]
    imag_part = product[:, :, 0, :, NS:] - product[:, :, 1, :, :NS]
    return jnp.concatenate([real_part, imag_part], axis=-1)


def reference(trace_map, interior_map, excitation, receiver_data, shot_index):
    trace_full = trace_map.astype(jnp.float32)
    interior_full = interior_map.astype(jnp.float32)
    sources = jnp.take(excitation, shot_index, axis=4).reshape(FREQS, S, K, 2 * NS)
    data_front = jnp.take(receiver_data, shot_index, axis=4).reshape(FREQS, S, K, 2 * NS)
    offset = GY + 1
    forward = sources
    adjoint = data_front
    for sweep_step in range(TICKS):
        grid_fwd = jnp.roll(forward, offset, axis=1).reshape(FREQS, GX, GY, K, 2 * NS).astype(jnp.float32)
        left_in = jnp.concatenate([jnp.zeros_like(grid_fwd[:, :, :1]), grid_fwd[:, :, :-1]], axis=2)
        up_in = jnp.concatenate([jnp.zeros_like(grid_fwd[:, :1]), grid_fwd[:, :-1]], axis=1)
        forward_in = jnp.roll((left_in + up_in).astype(jnp.bfloat16).reshape(FREQS, S, K, 2 * NS), -offset, axis=1)
        grid_adj = jnp.roll(adjoint, offset, axis=1).reshape(FREQS, GX, GY, K, 2 * NS).astype(jnp.float32)
        right_in = jnp.concatenate([grid_adj[:, :, 1:], jnp.zeros_like(grid_adj[:, :, :1])], axis=2)
        down_in = jnp.concatenate([grid_adj[:, 1:], jnp.zeros_like(grid_adj[:, :1])], axis=1)
        adjoint_in = jnp.roll((right_in + down_in).astype(jnp.bfloat16).reshape(FREQS, S, K, 2 * NS), -offset, axis=1)
        forward = (sources.astype(jnp.float32) + forward_apply(trace_full, forward_in)).astype(jnp.bfloat16)
        adjoint = (data_front.astype(jnp.float32) + adjoint_apply(trace_full, adjoint_in)).astype(jnp.bfloat16)
    wave = forward_apply(interior_full, forward).astype(jnp.bfloat16)
    back = forward_apply(interior_full, adjoint).astype(jnp.bfloat16)
    scale = (2.0 * NS * FREQS) ** -0.5
    image = jnp.einsum("fsam,fscm->sac", wave.astype(jnp.float32), back.astype(jnp.float32)) * scale
    return image
```

```python
import functools

import jax
import jax.numpy as jnp
import numpy as np
from jax import lax
from jax.sharding import PartitionSpec as P

GY = 4
TICKS = 6


def sweep_plan(total, sub_local, ticks, backward):
    rows = total // GY
    offset = GY + 1
    devices = total // sub_local

    def parents(g):
        out = []
        col, row = g % GY, g // GY
        if backward:
            if col != GY - 1:
                out.append(g + 1)
            if row != rows - 1:
                out.append(g + GY)
        else:
            if col != 0:
                out.append(g - 1)
            if row != 0:
                out.append(g - GY)
        return out

    def place(g):
        s = (g - offset) % total
        return s // sub_local, s % sub_local

    def depth(g):
        col, row = g % GY, g // GY
        return (GY - 1 - col) + (rows - 1 - row) if backward else col + row

    needed = {t: set() for t in range(ticks + 2)}
    for t in range(ticks, 0, -1):
        for g in range(total):
            if min(depth(g), ticks) == t:
                needed[t].add(g)
        for g in needed[t + 1]:
            for p in parents(g):
                if depth(p) >= t:
                    needed[t].add(p)
    plan = []
    for t in range(1, ticks + 1):
        permutes = []
        active = np.zeros((devices, sub_local), bool)
        local = np.zeros((devices, sub_local, sub_local), np.float32)
        sources = []
        for g in sorted(needed[t]):
            dev, slot = place(g)
            active[dev, slot] = True
            for p in parents(g):
                pdev, pslot = place(p)
                if pdev == dev:
                    local[dev, slot, pslot] = 1
                    continue
                for permute in permutes:
                    if permute["pairs"].get(pdev) == dev and permute["slot"][pdev] == pslot:
                        break
                else:
                    for permute in permutes:
                        if pdev not in permute["pairs"] and dev not in permute["pairs"].values():
                            break
                    else:
                        permute = {
                            "pairs": {},
                            "slot": np.zeros(devices, np.int32),
                            "use": np.zeros((devices, sub_local), np.float32),
                        }
                        permutes.append(permute)
                    permute["pairs"][pdev] = dev
                    permute["slot"][pdev] = pslot
                permute["use"][dev, slot] = 1
        plan.append({"permutes": permutes, "active": active, "local": local})
    return plan


def forward_apply(maps, front, shots):
    product = jnp.einsum("sckm,smn->sckn", maps, front, preferred_element_type=jnp.float32)
    real_part = product[:, 0, :, :shots] - product[:, 1, :, shots:]
    imag_part = product[:, 0, :, shots:] + product[:, 1, :, :shots]
    return jnp.concatenate([real_part, imag_part], axis=-1)


def adjoint_apply(maps, front, shots):
    product = jnp.einsum("sckm,skn->scmn", maps, front, preferred_element_type=jnp.float32)
    real_part = product[:, 0, :, :shots] + product[:, 1, :, shots:]
    imag_part = product[:, 0, :, shots:] - product[:, 1, :, :shots]
    return jnp.concatenate([real_part, imag_part], axis=-1)


def pick_shots(table, chooser, shape_out):
    picked = jnp.einsum("fsxcb,bn->fsxcn", table, chooser, preferred_element_type=jnp.float32)
    return picked.astype(jnp.bfloat16).reshape(shape_out)


def mine(table, device):
    return lax.dynamic_index_in_dim(jnp.asarray(table), device, 0, keepdims=False)


def gather_inputs(step, front, device):
    sub_local = front.shape[0]
    received = []
    for permute in step["permutes"]:
        slots = permute["slot"]
        senders = sorted(permute["pairs"])
        if len({int(slots[d]) for d in senders}) == 1:
            payload = front[int(slots[senders[0]])]
        else:
            payload = lax.dynamic_index_in_dim(front, mine(slots, device), 0, keepdims=False)
        received.append(lax.ppermute(payload, "sub", sorted(permute["pairs"].items())))

    def combine():
        total = [jnp.zeros(front.shape[1:], jnp.float32) for _ in range(sub_local)]
        for permute, value in zip(step["permutes"], received):
            use = mine(permute["use"], device)
            for s in range(sub_local):
                total[s] += value.astype(jnp.float32) * use[s]
        local = mine(step["local"], device)
        for s in range(sub_local):
            for r in range(sub_local):
                if step["local"][:, s, r].any():
                    total[s] += front[r].astype(jnp.float32) * local[s, r]
        return jnp.stack(total).astype(jnp.bfloat16)

    return combine


def per_device(trace_map, interior_map, excitation, receiver_data, shot_index):
    freq_local = trace_map.shape[0]
    sub_local = trace_map.shape[1]
    width = trace_map.shape[3]
    shots = shot_index.shape[0]
    bank_size = excitation.shape[4]
    front_shape = (freq_local, sub_local, width, 2 * shots)
    chooser = (
        lax.broadcasted_iota(jnp.int32, (bank_size, shots), 0) == shot_index[None, :]
    ).astype(jnp.bfloat16)
    sources = pick_shots(excitation, chooser, front_shape)
    data_front = pick_shots(receiver_data, chooser, front_shape)
    device = lax.axis_index("sub")
    total_subs = sub_local * lax.axis_size("sub")
    plans = [sweep_plan(total_subs, sub_local, TICKS, backward) for backward in (False, True)]
    origin = (sources, data_front)
    apply = (forward_apply, adjoint_apply)
    fronts = [[o[f] for f in range(freq_local)] for o in origin]
    for t in range(TICKS):
        pending = [
            [gather_inputs(plans[way][t], fronts[way][f], device) for way in range(2)]
            for f in range(freq_local)
        ]
        for f in range(freq_local):
            for way in range(2):
                active = mine(plans[way][t]["active"], device)[:, None, None]
                update = origin[way][f].astype(jnp.float32) + apply[way](
                    trace_map[f], pending[f][way](), shots
                )
                fronts[way][f] = jnp.where(active, update.astype(jnp.bfloat16), fronts[way][f])
    wave = [forward_apply(interior_map[f], fronts[0][f], shots).astype(jnp.bfloat16) for f in range(freq_local)]
    back = [forward_apply(interior_map[f], fronts[1][f], shots).astype(jnp.bfloat16) for f in range(freq_local)]
    wave, back = jnp.stack(wave), jnp.stack(back)
    groups = lax.axis_size("freq")
    core = lax.axis_index("freq")
    scale = (2.0 * shots * freq_local * groups) ** (-0.5)
    share = width // groups

    def rows_of(owner):
        return lax.dynamic_slice_in_dim(wave, owner * share, share, 2)

    image = jnp.einsum("fsam,fscm->sac", rows_of(core), back, preferred_element_type=jnp.float32)
    for shift in range(1, groups):
        ring = [(i, (i + shift) % groups) for i in range(groups)]
        their_wave = lax.ppermute(rows_of((core + shift) % groups), "freq", ring)
        their_back = lax.ppermute(back, "freq", ring)
        image += jnp.einsum("fsam,fscm->sac", their_wave, their_back, preferred_element_type=jnp.float32)
    return image * scale


def solution(mesh):
    placed = (
        P("freq", ("survey", "sub"), None, None, None),
        P("freq", ("survey", "sub"), None, None, None),
        P("freq", ("survey", "sub"), None, None, None),
        P("freq", ("survey", "sub"), None, None, None),
        P("survey"),
    )
    return jax.shard_map(
        per_device,
        mesh=mesh,
        in_specs=placed,
        out_specs=P(("survey", "sub"), "freq", None),
        check_vma=False,
    )
```

```python
import functools

import jax
import jax.numpy as jnp
import numpy as np
from jax import lax
from jax.experimental import pallas as pl
from jax.experimental.pallas import tpu as pltpu
from jax.sharding import PartitionSpec as P

GY = 4
TICKS = 6
BF16 = jnp.bfloat16
F32 = jnp.float32
TIMES = (((1,), (0,)), ((), ()))
TIMES_TRANSPOSED = (((1,), (1,)), ((), ()))
TRANSPOSED_TIMES = (((0,), (0,)), ((), ()))
VMEM_LIMIT = 24 * 1024 * 1024


class Grid:
    def __init__(self, total, sub_local):
        self.total, self.sub_local = total, sub_local
        self.devices, self.rows = total // sub_local, total // GY

    def place(self, g):
        s = (g - GY - 1) % self.total
        return s // self.sub_local, s % self.sub_local

    def parents(self, way, g):
        row, col = g // GY, g % GY
        if way == 0:
            return [g - 1] * (col != 0) + [g - GY] * (row != 0)
        return [g + 1] * (col != GY - 1) + [g + GY] * (row != self.rows - 1)

    def depth(self, way, g):
        row, col = g // GY, g % GY
        return row + col if way == 0 else self.rows - 1 - row + GY - 1 - col


def tick_program(grid, chunks):
    deepest = grid.rows + GY - 2
    program = []

    def sends(way, chunk, tick):
        permutes = []
        for g in range(grid.total):
            if grid.depth(way, g) != tick:
                continue
            here = grid.place(g)[0]
            for p in grid.parents(way, g):
                there = grid.place(p)[0]
                message = (way, chunk, p, there, here)
                if there == here or any(message in permute for permute in permutes):
                    continue
                for permute in permutes:
                    if all(m[3] != there and m[4] != here for m in permute):
                        permute.append(message)
                        break
                else:
                    permutes.append([message])
        program.extend(("send", permute) for permute in permutes)

    chains = [(way, chunk) for chunk in range(chunks) for way in range(2)]
    for way, chunk in chains:
        sends(way, chunk, 1)
    for tick in range(1, deepest + 1):
        for way, chunk in chains:
            nodes = [
                (g, grid.place(g)[0], tuple(grid.parents(way, g)))
                for g in range(grid.total)
                if grid.depth(way, g) == tick
            ]
            program.append(("compute", way, chunk, nodes))
            sends(way, chunk, tick + 1)
    return program


def bits(devices):
    return sum(1 << d for d in devices)


def flag(mask, device):
    return ((mask >> device) & 1) == 1


def apply_map(way, front, real_map, imag_map, shots):
    dims = TIMES_TRANSPOSED if way == 0 else TIMES
    by_real = lax.dot_general(front, real_map, dims, preferred_element_type=F32)
    by_imag = lax.dot_general(front, imag_map, dims, preferred_element_type=F32)
    if way == 0:
        return by_real[:shots] - by_imag[shots:], by_real[shots:] + by_imag[:shots]
    return by_real[:shots] + by_imag[shots:], by_real[shots:] - by_imag[:shots]


def compute_step(way, chunk, steps, device, maps, origin, arrays, shots):
    width = origin.shape[-1]

    def kernel(device_ref, maps_ref, origin_ref, *refs):
        ins, outs, total = refs[: len(arrays)], refs[len(arrays) : -1], refs[-1]
        me = device_ref[0]
        for out, step in zip(outs, steps):
            everyone = bits(step["slot"])

            @pl.when(flag(everyone, me))
            def _():
                sources = [(ins[i], mask) for i, mask in step["arrays"].items()]
                sources += [(outs[i], mask) for i, mask in step["earlier"].items()]
                if all(mask == everyone for _, mask in sources):
                    front = sources[0][0][...]
                    if len(sources) > 1:
                        front = sum((ref[...].astype(F32) for ref, _ in sources[1:]), front.astype(F32)).astype(BF16)
                else:
                    total[...] = jnp.zeros_like(total)
                    for ref, mask in sources:

                        @pl.when(flag(mask, me))
                        def _(ref=ref):
                            total[...] += ref[...].astype(F32)

                    front = total[...].astype(BF16)
                slot = jnp.int32(0)
                for s in range(1, origin_ref.shape[1]):
                    slot += s * ((bits([d for d, own in step["slot"].items() if own == s]) >> me) & 1)
                real_part, imag_part = apply_map(way, front, maps_ref[chunk, slot, 0], maps_ref[chunk, slot, 1], shots)
                start = origin_ref[chunk, slot].astype(F32)
                out[:shots] = (start[:shots] + real_part).astype(BF16)
                out[shots:] = (start[shots:] + imag_part).astype(BF16)

    vmem = pl.BlockSpec(memory_space=pltpu.VMEM)
    return pl.pallas_call(
        kernel,
        out_shape=[jax.ShapeDtypeStruct((2 * shots, width), BF16)] * len(steps),
        in_specs=[pl.BlockSpec(memory_space=pltpu.SMEM)] + [vmem] * (2 + len(arrays)),
        out_specs=[vmem] * len(steps),
        scratch_shapes=[pltpu.VMEM((2 * shots, width), F32)],
        compiler_params=pltpu.CompilerParams(vmem_limit_bytes=VMEM_LIMIT),
        cost_estimate=pl.CostEstimate(flops=8 * shots * width * width, bytes_accessed=1 << 20, transcendentals=0),
        name=f"front_{way}_{chunk}",
    )(device, maps, origin, *arrays)


def sweep(program, grid, device, maps, origins, shots):
    chunks = maps.shape[0]
    arrays, where, holders = [], {}, {}

    def keep(value):
        arrays.append(value)
        return len(arrays) - 1

    for way in range(2):
        for chunk in range(chunks):
            for g in range(grid.total):
                if grid.depth(way, g) == 0:
                    dev, slot = grid.place(g)
                    where[way, chunk, g, dev] = index = keep(origins[way][chunk, slot])
                    holders[way, chunk, g] = index
    for kind, *body in program:
        if kind == "send":
            (messages,) = body
            by_array = {}
            for way, chunk, value, here, there in messages:
                by_array.setdefault(where[way, chunk, value, here], []).append(here)
            payload = None
            for index, senders in by_array.items():
                if payload is None:
                    payload = arrays[index]
                else:
                    payload = jnp.where(flag(bits(senders), device[0]), arrays[index], payload)
            index = keep(lax.ppermute(payload, "sub", sorted((m[3], m[4]) for m in messages)))
            for way, chunk, value, _, there in messages:
                where[way, chunk, value, there] = index
            continue
        way, chunk, nodes = body
        steps, operands, made, count = [], [], {}, {}
        for value, dev, inputs in nodes:
            position = count.get(dev, 0)
            count[dev] = position + 1
            if position == len(steps):
                steps.append({"slot": {}, "arrays": {}, "earlier": {}})
            step = steps[position]
            step["slot"][dev] = grid.place(value)[1]
            for v in inputs:
                if (v, dev) in made:
                    earlier = made[v, dev]
                    step["earlier"][earlier] = step["earlier"].get(earlier, 0) | 1 << dev
                else:
                    index = where[way, chunk, v, dev]
                    if index not in operands:
                        operands.append(index)
                    index = operands.index(index)
                    step["arrays"][index] = step["arrays"].get(index, 0) | 1 << dev
            made[value, dev] = position
        results = compute_step(
            way, chunk, steps, device, maps, origins[way], [arrays[i] for i in operands], shots
        )
        kept = [keep(r) for r in results]
        for (value, dev), position in made.items():
            where[way, chunk, value, dev] = kept[position]
            holders[way, chunk, value] = kept[position]
    finished = {}
    for (way, chunk, g), index in holders.items():
        dev, slot = grid.place(g)
        finished.setdefault((way, chunk, slot), {}).setdefault(index, []).append(dev)
    return {key: [(arrays[i], bits(devs)) for i, devs in found.items()] for key, found in finished.items()}


def interior_step(finished, device, maps, shots):
    freqs, subs, _, width, _ = maps.shape
    columns = 2 * shots
    arrays, choices = [], {}
    for key, found in finished.items():
        choices[key] = [(len(arrays) + i, mask) for i, (_, mask) in enumerate(found)]
        arrays += [a for a, _ in found]

    def kernel(device_ref, maps_ref, *refs):
        ins, (wave, back), both = refs[: len(arrays)], refs[len(arrays) : -1], refs[-1]
        me = device_ref[0]
        for f in range(freqs):
            for s in range(subs):
                for way in range(2):
                    for i, mask in choices[way, f, s]:

                        @pl.when(flag(mask, me))
                        def _(i=i, way=way):
                            both[way * columns : (way + 1) * columns] = ins[i][...]

                front = both[...]
                by_real = lax.dot_general(front, maps_ref[f, s, 0], TIMES_TRANSPOSED, preferred_element_type=F32)
                by_imag = lax.dot_general(front, maps_ref[f, s, 1], TIMES_TRANSPOSED, preferred_element_type=F32)
                for way, out in enumerate((wave, back)):
                    a, b = way * columns, way * columns + shots
                    out[f, s, :shots] = (by_real[a : a + shots] - by_imag[b : b + shots]).astype(BF16)
                    out[f, s, shots:] = (by_real[b : b + shots] + by_imag[a : a + shots]).astype(BF16)

    vmem = pl.BlockSpec(memory_space=pltpu.VMEM)
    shape = jax.ShapeDtypeStruct((freqs, subs, columns, width), BF16)
    return pl.pallas_call(
        kernel,
        out_shape=[shape, shape],
        in_specs=[pl.BlockSpec(memory_space=pltpu.SMEM)] + [vmem] * (1 + len(arrays)),
        out_specs=[vmem, vmem],
        scratch_shapes=[pltpu.VMEM((2 * columns, width), BF16)],
        compiler_params=pltpu.CompilerParams(vmem_limit_bytes=VMEM_LIMIT),
        name="interior",
    )(device, maps, *arrays)


def image_step(waves, backs, scale):
    freqs, subs, _, share = waves[0].shape
    width = backs[0].shape[-1]
    groups = len(waves)

    def kernel(*refs):
        out = refs[-1]
        for s in range(subs):
            rows = jnp.concatenate([refs[g][f, s] for g in range(groups) for f in range(freqs)], axis=0)
            points = jnp.concatenate([refs[groups + g][f, s] for g in range(groups) for f in range(freqs)], axis=0)
            out[s] = lax.dot_general(rows, points, TRANSPOSED_TIMES, preferred_element_type=F32) * scale

    vmem = pl.BlockSpec(memory_space=pltpu.VMEM)
    return pl.pallas_call(
        kernel,
        out_shape=jax.ShapeDtypeStruct((subs, share, width), F32),
        in_specs=[vmem] * (2 * groups),
        out_specs=vmem,
        compiler_params=pltpu.CompilerParams(vmem_limit_bytes=VMEM_LIMIT),
        name="image",
    )(*waves, *backs)


def pick_shots(table, chooser):
    freqs, subs, width, _, _ = table.shape
    picked = jnp.einsum("fsxcb,bn->fscnx", table, chooser, preferred_element_type=F32)
    return picked.astype(BF16).reshape(freqs, subs, -1, width)


def make_image(wave, back, scale):
    width = wave.shape[-1]
    groups = lax.axis_size("freq")
    core = lax.axis_index("freq")
    share = width // groups

    def rows_of(owner):
        return lax.dynamic_slice_in_dim(wave, owner * share, share, 3)

    waves, backs = [rows_of(core)], [back]
    for shift in range(1, groups):
        ring = [(i, (i + shift) % groups) for i in range(groups)]
        waves.append(lax.ppermute(rows_of((core + shift) % groups), "freq", ring))
        backs.append(lax.ppermute(back, "freq", ring))
    return image_step(waves, backs, scale)


def per_device(trace_map, interior_map, excitation, receiver_data, shot_index):
    freq_local, sub_local = trace_map.shape[:2]
    shots = shot_index.shape[0]
    bank_size = excitation.shape[4]
    chooser = (
        lax.broadcasted_iota(jnp.int32, (bank_size, shots), 0) == shot_index[None, :]
    ).astype(BF16)
    origins = (pick_shots(excitation, chooser), pick_shots(receiver_data, chooser))
    device = lax.axis_index("sub").astype(jnp.int32).reshape(1)
    grid = Grid(sub_local * lax.axis_size("sub"), sub_local)
    scale = (2.0 * shots * freq_local * lax.axis_size("freq")) ** (-0.5)
    if grid.rows + GY - 2 <= TICKS:
        finished = sweep(tick_program(grid, freq_local), grid, device, trace_map, origins, shots)
    else:
        finished = jacobi(grid, device, trace_map, origins, shots)
    wave, back = interior_step(finished, device, interior_map, shots)
    return make_image(wave, back, scale)


def jacobi(grid, device, maps, origins, shots):
    chunks, subs = maps.shape[:2]
    reach = GY // subs
    count = grid.devices
    places = (device[0] * subs + jnp.arange(subs, dtype=jnp.int32) + GY + 1) % grid.total
    column, row = places % GY, places // GY

    def move(x, by):
        return lax.ppermute(x, "sub", [(i, (i + by) % count) for i in range(count)])

    def mask(flags):
        return flags.astype(F32)[None, :, None, None]

    forward, adjoint = origins
    for _ in range(TICKS):
        left = jnp.concatenate([move(forward[:, subs - 1 :], 1), forward[:, : subs - 1]], axis=1)
        above = move(forward, reach)
        right = jnp.concatenate([adjoint[:, 1:], move(adjoint[:, :1], -1)], axis=1)
        below = move(adjoint, -reach)
        forward_in = left.astype(F32) * mask(column != 0) + above.astype(F32) * mask(row != 0)
        adjoint_in = right.astype(F32) * mask(column != GY - 1) + below.astype(F32) * mask(row != grid.rows - 1)
        fronts = []
        for way, total in enumerate((forward_in, adjoint_in)):
            dims = "fsnm,fsckm->fscnk" if way == 0 else "fsnk,fsckm->fscnm"
            product = jnp.einsum(dims, total.astype(BF16), maps, preferred_element_type=F32)
            real, imag = product[:, :, 0], product[:, :, 1]
            sign = 1.0 if way == 0 else -1.0
            moved = jnp.concatenate(
                [
                    real[:, :, :shots] - sign * imag[:, :, shots:],
                    real[:, :, shots:] + sign * imag[:, :, :shots],
                ],
                axis=2,
            )
            fronts.append((origins[way].astype(F32) + moved).astype(BF16))
        forward, adjoint = fronts
    everyone = bits(range(count))
    return {
        (way, f, s): [(front[f, s], everyone)]
        for way, front in enumerate((forward, adjoint))
        for f in range(chunks)
        for s in range(subs)
    }


def solution(mesh):
    placed = (
        P("freq", ("survey", "sub"), None, None, None),
        P("freq", ("survey", "sub"), None, None, None),
        P("freq", ("survey", "sub"), None, None, None),
        P("freq", ("survey", "sub"), None, None, None),
        P("survey"),
    )
    return jax.shard_map(
        per_device,
        mesh=mesh,
        in_specs=placed,
        out_specs=P(("survey", "sub"), "freq", None),
        check_vma=False,
    )
```

```python
import functools

import jax
import jax.numpy as jnp
import numpy as np
from jax import lax
from jax.experimental import pallas as pl
from jax.experimental.pallas import tpu as pltpu
from jax.sharding import PartitionSpec as P

GY = 4
TICKS = 6
CHUNKS = 1
BF16 = jnp.bfloat16
F32 = jnp.float32
TIMES = (((1,), (0,)), ((), ()))
TIMES_TRANSPOSED = (((1,), (1,)), ((), ()))
TRANSPOSED_TIMES = (((0,), (0,)), ((), ()))
VMEM_LIMIT = 24 * 1024 * 1024


class Grid:
    def __init__(self, total, sub_local):
        self.total, self.sub_local = total, sub_local
        self.devices, self.rows = total // sub_local, total // GY

    def place(self, g):
        s = (g - GY - 1) % self.total
        return s // self.sub_local, s % self.sub_local

    def parents(self, way, g):
        row, col = g // GY, g % GY
        if way == 0:
            return [g - 1] * (col != 0) + [g - GY] * (row != 0)
        return [g + 1] * (col != GY - 1) + [g + GY] * (row != self.rows - 1)

    def depth(self, way, g):
        row, col = g // GY, g % GY
        return row + col if way == 0 else self.rows - 1 - row + GY - 1 - col


def tick_program(grid, chunks):
    deepest = grid.rows + GY - 2
    program = []

    def sends(way, chunk, tick):
        permutes = []
        for g in range(grid.total):
            if grid.depth(way, g) != tick:
                continue
            here = grid.place(g)[0]
            for p in grid.parents(way, g):
                there = grid.place(p)[0]
                message = (way, chunk, p, there, here)
                if there == here or any(message in permute for permute in permutes):
                    continue
                for permute in permutes:
                    if all(m[3] != there and m[4] != here for m in permute):
                        permute.append(message)
                        break
                else:
                    permutes.append([message])
        program.extend(("send", permute) for permute in permutes)

    chains = [(way, chunk) for chunk in range(chunks) for way in range(2)]
    for way, chunk in chains:
        sends(way, chunk, 1)
    for tick in range(1, deepest + 1):
        for way, chunk in chains:
            nodes = [
                (g, grid.place(g)[0], tuple(grid.parents(way, g)))
                for g in range(grid.total)
                if grid.depth(way, g) == tick
            ]
            program.append(("compute", way, chunk, nodes))
            sends(way, chunk, tick + 1)
    return program


def bits(devices):
    return sum(1 << d for d in devices)


def flag(mask, device):
    return ((mask >> device) & 1) == 1


def apply_map(way, front, real_map, imag_map, shots):
    dims = TIMES_TRANSPOSED if way == 0 else TIMES
    by_real = lax.dot_general(front, real_map, dims, preferred_element_type=F32)
    by_imag = lax.dot_general(front, imag_map, dims, preferred_element_type=F32)
    if way == 0:
        return by_real[:shots] - by_imag[shots:], by_real[shots:] + by_imag[:shots]
    return by_real[:shots] + by_imag[shots:], by_real[shots:] - by_imag[:shots]


def compute_step(way, chunk, steps, device, maps, origin, arrays, shots):
    width = origin.shape[-1]
    shape = (len(chunk), 2 * shots, width)

    def kernel(device_ref, maps_ref, origin_ref, *refs):
        ins, outs, total = refs[: len(arrays)], refs[len(arrays) : -1], refs[-1]
        me = device_ref[0]
        for out, step in zip(outs, steps):
            everyone = bits(step["slot"])

            @pl.when(flag(everyone, me))
            def _():
                sources = [(ins[i], mask) for i, mask in step["arrays"].items()]
                sources += [(outs[i], mask) for i, mask in step["earlier"].items()]
                if all(mask == everyone for _, mask in sources):
                    front = sources[0][0][...]
                    if len(sources) > 1:
                        front = sum((ref[...].astype(F32) for ref, _ in sources[1:]), front.astype(F32)).astype(BF16)
                else:
                    total[...] = jnp.zeros_like(total)
                    for ref, mask in sources:

                        @pl.when(flag(mask, me))
                        def _(ref=ref):
                            total[...] += ref[...].astype(F32)

                    front = total[...].astype(BF16)
                slot = jnp.int32(0)
                for s in range(1, origin_ref.shape[1]):
                    slot += s * ((bits([d for d, own in step["slot"].items() if own == s]) >> me) & 1)
                for i, f in enumerate(chunk):
                    real_part, imag_part = apply_map(way, front[i], maps_ref[f, slot, 0], maps_ref[f, slot, 1], shots)
                    start = origin_ref[f, slot].astype(F32)
                    out[i, :shots] = (start[:shots] + real_part).astype(BF16)
                    out[i, shots:] = (start[shots:] + imag_part).astype(BF16)

    vmem = pl.BlockSpec(memory_space=pltpu.VMEM)
    return pl.pallas_call(
        kernel,
        out_shape=[jax.ShapeDtypeStruct(shape, BF16)] * len(steps),
        in_specs=[pl.BlockSpec(memory_space=pltpu.SMEM)] + [vmem] * (2 + len(arrays)),
        out_specs=[vmem] * len(steps),
        scratch_shapes=[pltpu.VMEM(shape, F32)],
        compiler_params=pltpu.CompilerParams(vmem_limit_bytes=VMEM_LIMIT),
        cost_estimate=pl.CostEstimate(flops=8 * shots * width * width, bytes_accessed=1 << 20, transcendentals=0),
        name=f"front_{way}_{chunk[0]}",
    )(device, maps, origin, *arrays)


def sweep(program, chunks, grid, device, maps, origins, shots):
    per_chunk = maps.shape[0] // chunks
    arrays, where, holders = [], {}, {}

    def keep(value):
        arrays.append(value)
        return len(arrays) - 1

    for way in range(2):
        for chunk in range(chunks):
            for g in range(grid.total):
                if grid.depth(way, g) == 0:
                    dev, slot = grid.place(g)
                    where[way, chunk, g, dev] = index = keep(origins[way][chunk * per_chunk : (chunk + 1) * per_chunk, slot])
                    holders[way, chunk, g] = index
    for kind, *body in program:
        if kind == "send":
            (messages,) = body
            by_array = {}
            for way, chunk, value, here, there in messages:
                by_array.setdefault(where[way, chunk, value, here], []).append(here)
            payload = None
            for index, senders in by_array.items():
                if payload is None:
                    payload = arrays[index]
                else:
                    payload = jnp.where(flag(bits(senders), device[0]), arrays[index], payload)
            index = keep(lax.ppermute(payload, "sub", sorted((m[3], m[4]) for m in messages)))
            for way, chunk, value, _, there in messages:
                where[way, chunk, value, there] = index
            continue
        way, chunk, nodes = body
        steps, operands, made, count = [], [], {}, {}
        for value, dev, inputs in nodes:
            position = count.get(dev, 0)
            count[dev] = position + 1
            if position == len(steps):
                steps.append({"slot": {}, "arrays": {}, "earlier": {}})
            step = steps[position]
            step["slot"][dev] = grid.place(value)[1]
            for v in inputs:
                if (v, dev) in made:
                    earlier = made[v, dev]
                    step["earlier"][earlier] = step["earlier"].get(earlier, 0) | 1 << dev
                else:
                    index = where[way, chunk, v, dev]
                    if index not in operands:
                        operands.append(index)
                    index = operands.index(index)
                    step["arrays"][index] = step["arrays"].get(index, 0) | 1 << dev
            made[value, dev] = position
        results = compute_step(
            way, range(chunk * per_chunk, (chunk + 1) * per_chunk), steps, device, maps, origins[way],
            [arrays[i] for i in operands], shots
        )
        kept = [keep(r) for r in results]
        for (value, dev), position in made.items():
            where[way, chunk, value, dev] = kept[position]
            holders[way, chunk, value] = kept[position]
    finished = {}
    for (way, chunk, g), index in holders.items():
        dev, slot = grid.place(g)
        for f in range(per_chunk):
            finished.setdefault((way, chunk * per_chunk + f, slot), {}).setdefault((index, f), []).append(dev)
    return {key: [(arrays[i], f, bits(devs)) for (i, f), devs in found.items()] for key, found in finished.items()}


def interior_step(finished, device, maps, shots):
    freqs, subs, _, width, _ = maps.shape
    columns = 2 * shots
    arrays, choices = [], {}
    for key, found in finished.items():
        choices[key] = []
        for array, f, mask in found:
            if not any(array is a for a in arrays):
                arrays.append(array)
            choices[key].append((next(i for i, a in enumerate(arrays) if a is array), f, mask))

    def kernel(device_ref, maps_ref, *refs):
        ins, (wave, back), both = refs[: len(arrays)], refs[len(arrays) : -1], refs[-1]
        me = device_ref[0]
        for f in range(freqs):
            for s in range(subs):
                for way in range(2):
                    for i, part, mask in choices[way, f, s]:

                        @pl.when(flag(mask, me))
                        def _(i=i, part=part, way=way):
                            both[way * columns : (way + 1) * columns] = ins[i][part]

                front = both[...]
                by_real = lax.dot_general(front, maps_ref[f, s, 0], TIMES_TRANSPOSED, preferred_element_type=F32)
                by_imag = lax.dot_general(front, maps_ref[f, s, 1], TIMES_TRANSPOSED, preferred_element_type=F32)
                for way, out in enumerate((wave, back)):
                    a, b = way * columns, way * columns + shots
                    out[f, s, :shots] = (by_real[a : a + shots] - by_imag[b : b + shots]).astype(BF16)
                    out[f, s, shots:] = (by_real[b : b + shots] + by_imag[a : a + shots]).astype(BF16)

    vmem = pl.BlockSpec(memory_space=pltpu.VMEM)
    shape = jax.ShapeDtypeStruct((freqs, subs, columns, width), BF16)
    return pl.pallas_call(
        kernel,
        out_shape=[shape, shape],
        in_specs=[pl.BlockSpec(memory_space=pltpu.SMEM)] + [vmem] * (1 + len(arrays)),
        out_specs=[vmem, vmem],
        scratch_shapes=[pltpu.VMEM((2 * columns, width), BF16)],
        compiler_params=pltpu.CompilerParams(vmem_limit_bytes=VMEM_LIMIT),
        name="interior",
    )(device, maps, *arrays)


def image_step(waves, backs, scale):
    freqs, subs, _, share = waves[0].shape
    width = backs[0].shape[-1]
    groups = len(waves)

    def kernel(*refs):
        out = refs[-1]
        for s in range(subs):
            rows = jnp.concatenate([refs[g][f, s] for g in range(groups) for f in range(freqs)], axis=0)
            points = jnp.concatenate([refs[groups + g][f, s] for g in range(groups) for f in range(freqs)], axis=0)
            out[s] = lax.dot_general(rows, points, TRANSPOSED_TIMES, preferred_element_type=F32) * scale

    vmem = pl.BlockSpec(memory_space=pltpu.VMEM)
    return pl.pallas_call(
        kernel,
        out_shape=jax.ShapeDtypeStruct((subs, share, width), F32),
        in_specs=[vmem] * (2 * groups),
        out_specs=vmem,
        compiler_params=pltpu.CompilerParams(vmem_limit_bytes=VMEM_LIMIT),
        name="image",
    )(*waves, *backs)


def pick_shots(table, chooser):
    freqs, subs, width, _, _ = table.shape
    picked = jnp.einsum("fsxcb,bn->fscnx", table, chooser, preferred_element_type=F32)
    return picked.astype(BF16).reshape(freqs, subs, -1, width)


def make_image(wave, back, scale):
    width = wave.shape[-1]
    groups = lax.axis_size("freq")
    core = lax.axis_index("freq")
    share = width // groups

    def rows_of(owner):
        return lax.dynamic_slice_in_dim(wave, owner * share, share, 3)

    waves, backs = [rows_of(core)], [back]
    for shift in range(1, groups):
        ring = [(i, (i + shift) % groups) for i in range(groups)]
        waves.append(lax.ppermute(rows_of((core + shift) % groups), "freq", ring))
        backs.append(lax.ppermute(back, "freq", ring))
    return image_step(waves, backs, scale)


def per_device(trace_map, interior_map, excitation, receiver_data, shot_index):
    freq_local, sub_local = trace_map.shape[:2]
    shots = shot_index.shape[0]
    bank_size = excitation.shape[4]
    chooser = (
        lax.broadcasted_iota(jnp.int32, (bank_size, shots), 0) == shot_index[None, :]
    ).astype(BF16)
    origins = (pick_shots(excitation, chooser), pick_shots(receiver_data, chooser))
    device = lax.axis_index("sub").astype(jnp.int32).reshape(1)
    grid = Grid(sub_local * lax.axis_size("sub"), sub_local)
    scale = (2.0 * shots * freq_local * lax.axis_size("freq")) ** (-0.5)
    if grid.rows + GY - 2 <= TICKS:
        finished = sweep(tick_program(grid, CHUNKS), CHUNKS, grid, device, trace_map, origins, shots)
    else:
        finished = jacobi(grid, device, trace_map, origins, shots)
    wave, back = interior_step(finished, device, interior_map, shots)
    return make_image(wave, back, scale)


def jacobi(grid, device, maps, origins, shots):
    chunks, subs = maps.shape[:2]
    reach = GY // subs
    count = grid.devices
    places = (device[0] * subs + jnp.arange(subs, dtype=jnp.int32) + GY + 1) % grid.total
    column, row = places % GY, places // GY

    def move(x, by):
        return lax.ppermute(x, "sub", [(i, (i + by) % count) for i in range(count)])

    def mask(flags):
        return flags.astype(F32)[None, :, None, None]

    forward, adjoint = origins
    for _ in range(TICKS):
        left = jnp.concatenate([move(forward[:, subs - 1 :], 1), forward[:, : subs - 1]], axis=1)
        above = move(forward, reach)
        right = jnp.concatenate([adjoint[:, 1:], move(adjoint[:, :1], -1)], axis=1)
        below = move(adjoint, -reach)
        forward_in = left.astype(F32) * mask(column != 0) + above.astype(F32) * mask(row != 0)
        adjoint_in = right.astype(F32) * mask(column != GY - 1) + below.astype(F32) * mask(row != grid.rows - 1)
        fronts = []
        for way, total in enumerate((forward_in, adjoint_in)):
            dims = "fsnm,fsckm->fscnk" if way == 0 else "fsnk,fsckm->fscnm"
            product = jnp.einsum(dims, total.astype(BF16), maps, preferred_element_type=F32)
            real, imag = product[:, :, 0], product[:, :, 1]
            sign = 1.0 if way == 0 else -1.0
            moved = jnp.concatenate(
                [
                    real[:, :, :shots] - sign * imag[:, :, shots:],
                    real[:, :, shots:] + sign * imag[:, :, :shots],
                ],
                axis=2,
            )
            fronts.append((origins[way].astype(F32) + moved).astype(BF16))
        forward, adjoint = fronts
    everyone = bits(range(count))
    return {
        (way, f, s): [(front[:, s], f, everyone)]
        for way, front in enumerate((forward, adjoint))
        for f in range(chunks)
        for s in range(subs)
    }


def solution(mesh):
    placed = (
        P("freq", ("survey", "sub"), None, None, None),
        P("freq", ("survey", "sub"), None, None, None),
        P("freq", ("survey", "sub"), None, None, None),
        P("freq", ("survey", "sub"), None, None, None),
        P("survey"),
    )
    return jax.shard_map(
        per_device,
        mesh=mesh,
        in_specs=placed,
        out_specs=P(("survey", "sub"), "freq", None),
        check_vma=False,
    )
```

```python
import functools

import jax
import jax.numpy as jnp
import numpy as np
from jax import lax
from jax.experimental import pallas as pl
from jax.experimental.pallas import tpu as pltpu
from jax.sharding import PartitionSpec as P

GY = 4
TICKS = 6
BF16 = jnp.bfloat16
F32 = jnp.float32
TIMES = (((1,), (0,)), ((), ()))
TIMES_TRANSPOSED = (((1,), (1,)), ((), ()))
TRANSPOSED_TIMES = (((0,), (0,)), ((), ()))
VMEM_LIMIT = 12 * 1024 * 1024
CHUNKS_OF_4X4 = 1
PROGRAM_OF_4X4 = (
    (0, ((1, 0, 15, 5, 4),)),
    (0, ((1, 0, 15, 5, 3),)),
    (0, ((0, 0, 0, 5, 6),)),
    (1, 1, 0, ((14, 4),)),
    (0, ((1, 0, 14, 4, 2),)),
    (0, ((0, 0, 0, 5, 7),)),
    (1, 0, 0, ((1, 6), (2, 6))),
    (1, 1, 0, ((11, 3),)),
    (0, ((1, 0, 11, 3, 2), (0, 0, 2, 6, 7))),
    (0, ((1, 0, 11, 3, 1),)),
    (1, 0, 0, ((4, 7),)),
    (0, ((0, 0, 4, 7, 1),)),
    (1, 1, 0, ((7, 1), (13, 4))),
    (0, ((1, 0, 7, 1, 0),)),
    (0, ((1, 0, 7, 1, 7),)),
    (1, 0, 0, ((8, 1),)),
    (0, ((1, 0, 13, 4, 2),)),
    (1, 1, 0, ((10, 2),)),
    (0, ((1, 0, 10, 2, 0),)),
    (1, 1, 0, ((3, 7),)),
    (0, ((1, 0, 13, 2, 3),)),
    (1, 1, 0, ((9, 2),)),
    (0, ((1, 0, 9, 2, 0),)),
    (0, ((0, 0, 4, 1, 0),)),
    (1, 1, 0, ((6, 0),)),
    (0, ((0, 0, 1, 6, 0), (1, 0, 6, 0, 6), (0, 0, 8, 1, 3))),
    (1, 1, 0, ((12, 3), (5, 0))),
    (0, ((1, 0, 5, 0, 6), (1, 0, 12, 3, 1))),
    (0, ((1, 0, 9, 0, 1), (0, 0, 2, 6, 0), (1, 0, 3, 7, 6))),
    (1, 0, 0, ((3, 7), (5, 0))),
    (0, ((0, 0, 5, 0, 2),)),
    (0, ((0, 0, 8, 3, 2), (0, 0, 3, 7, 1))),
    (1, 0, 0, ((12, 3), (6, 0))),
    (0, ((0, 0, 6, 0, 2),)),
    (0, ((0, 0, 6, 0, 1),)),
    (1, 1, 0, ((8, 1),)),
    (1, 1, 0, ((2, 6), (1, 6))),
    (0, ((1, 0, 8, 1, 7), (0, 0, 12, 3, 4))),
    (1, 0, 0, ((9, 2),)),
    (1, 0, 0, ((7, 1),)),
    (0, ((0, 0, 7, 1, 3), (1, 0, 1, 6, 5), (0, 0, 9, 2, 4))),
    (1, 0, 0, ((10, 2),)),
    (0, ((0, 0, 10, 2, 4),)),
    (0, ((0, 0, 10, 2, 3), (1, 0, 5, 6, 7))),
    (1, 0, 0, ((11, 3),)),
    (0, ((0, 0, 11, 3, 5),)),
    (1, 1, 0, ((4, 7),)),
    (1, 0, 0, ((13, 4),)),
    (1, 0, 0, ((14, 4),)),
    (0, ((1, 0, 4, 7, 5),)),
    (0, ((0, 0, 14, 4, 5),)),
    (1, 1, 0, ((0, 5),)),
    (1, 0, 0, ((15, 5),)),
)


class Grid:
    def __init__(self, total, sub_local):
        self.total, self.sub_local = total, sub_local
        self.devices, self.rows = total // sub_local, total // GY

    def place(self, g):
        s = (g - GY - 1) % self.total
        return s // self.sub_local, s % self.sub_local

    def parents(self, way, g):
        row, col = g // GY, g % GY
        if way == 0:
            return [g - 1] * (col != 0) + [g - GY] * (row != 0)
        return [g + 1] * (col != GY - 1) + [g + GY] * (row != self.rows - 1)

    def depth(self, way, g):
        row, col = g // GY, g % GY
        return row + col if way == 0 else self.rows - 1 - row + GY - 1 - col


def tick_program(grid, chunks):
    deepest = grid.rows + GY - 2
    program = []

    def sends(way, chunk, tick):
        permutes = []
        for g in range(grid.total):
            if grid.depth(way, g) != tick:
                continue
            here = grid.place(g)[0]
            for p in grid.parents(way, g):
                there = grid.place(p)[0]
                message = (way, chunk, p, there, here)
                if there == here or any(message in permute for permute in permutes):
                    continue
                for permute in permutes:
                    if all(m[3] != there and m[4] != here for m in permute):
                        permute.append(message)
                        break
                else:
                    permutes.append([message])
        program.extend(("send", permute) for permute in permutes)

    chains = [(way, chunk) for chunk in range(chunks) for way in range(2)]
    for way, chunk in chains:
        sends(way, chunk, 1)
    for tick in range(1, deepest + 1):
        for way, chunk in chains:
            nodes = [(g, grid.place(g)[0]) for g in range(grid.total) if grid.depth(way, g) == tick]
            program.append(("compute", way, chunk, nodes))
            sends(way, chunk, tick + 1)
    return program


def bits(devices):
    return sum(1 << d for d in devices)


def flag(mask, device):
    return ((mask >> device) & 1) == 1


def apply_map(way, front, real_map, imag_map, shots):
    dims = TIMES_TRANSPOSED if way == 0 else TIMES
    by_real = lax.dot_general(front, real_map, dims, preferred_element_type=F32)
    by_imag = lax.dot_general(front, imag_map, dims, preferred_element_type=F32)
    if way == 0:
        return by_real[:shots] - by_imag[shots:], by_real[shots:] + by_imag[:shots]
    return by_real[:shots] + by_imag[shots:], by_real[shots:] - by_imag[:shots]


def compute_step(way, chunk, steps, place, groups, maps, origin, arrays, before, shots):
    width = origin.shape[-1]
    shape = (len(chunk), 2 * shots, width)

    def kernel(place_ref, maps_ref, origin_ref, _, *refs):
        ins, outs, total = refs[: len(arrays)], refs[len(arrays) : -1], refs[-1]
        me = place_ref[0] // groups
        for out, step in zip(outs, steps):
            everyone = bits(step["slot"])

            @pl.when(flag(everyone, me))
            def _():
                sources = [(ins[i], part, mask) for (i, part), mask in step["arrays"].items()]
                sources += [(outs[i], 0, mask) for i, mask in step["earlier"].items()]
                if all(mask == everyone for _, _, mask in sources):
                    first, part, _ = sources[0]
                    front = first[pl.ds(part, len(chunk))]
                    if len(sources) > 1:
                        front = front.astype(F32)
                        for ref, part, _ in sources[1:]:
                            front += ref[pl.ds(part, len(chunk))].astype(F32)
                        front = front.astype(BF16)
                else:
                    total[...] = jnp.zeros_like(total)
                    for ref, part, mask in sources:

                        @pl.when(flag(mask, me))
                        def _(ref=ref, part=part):
                            total[...] += ref[pl.ds(part, len(chunk))].astype(F32)

                    front = total[...].astype(BF16)
                sums = step["sums"]
                if sums:

                    @pl.when(flag(bits(sums), me))
                    def _():
                        out[...] = front

                if len(sums) == len(step["slot"]):
                    return

                @pl.when(flag(everyone & ~bits(sums), me))
                def _():
                    slot = jnp.int32(0)
                    for s in range(1, origin_ref.shape[1]):
                        slot += s * ((bits([d for d, own in step["slot"].items() if own == s]) >> me) & 1)
                    for i, f in enumerate(chunk):
                        real_part, imag_part = apply_map(way, front[i], maps_ref[f, slot, 0], maps_ref[f, slot, 1], shots)
                        start = origin_ref[f, slot].astype(F32)
                        out[i, :shots] = (start[:shots] + real_part).astype(BF16)
                        out[i, shots:] = (start[shots:] + imag_part).astype(BF16)

    vmem = pl.BlockSpec(memory_space=pltpu.VMEM)
    return pl.pallas_call(
        kernel,
        out_shape=[jax.ShapeDtypeStruct(shape, BF16)] * len(steps),
        in_specs=[pl.BlockSpec(memory_space=pltpu.SMEM), vmem, vmem, pl.BlockSpec(memory_space=pl.ANY)]
        + [vmem] * len(arrays),
        out_specs=[vmem] * len(steps),
        scratch_shapes=[pltpu.VMEM(shape, F32)],
        compiler_params=pltpu.CompilerParams(vmem_limit_bytes=VMEM_LIMIT),
        cost_estimate=pl.CostEstimate(flops=8 * shots * width * width, bytes_accessed=1 << 20, transcendentals=0),
        name=f"front_{way}_{chunk[0]}",
    )(place, maps, origin, before, *arrays)


def choose_step(found, place, groups):
    def kernel(place_ref, *refs):
        me = place_ref[0] // groups
        for ref, (_, mask) in zip(refs, found):

            @pl.when(flag(mask, me))
            def _(ref=ref):
                refs[-1][...] = ref[...]

    vmem = pl.BlockSpec(memory_space=pltpu.VMEM)
    return pl.pallas_call(
        kernel,
        out_shape=jax.ShapeDtypeStruct(found[0][0].shape, BF16),
        in_specs=[pl.BlockSpec(memory_space=pltpu.SMEM)] + [vmem] * len(found),
        out_specs=vmem,
        compiler_params=pltpu.CompilerParams(vmem_limit_bytes=VMEM_LIMIT),
        name="choose",
    )(place, *[array for array, _ in found])


def sweep(program, chunks, grid, place, groups, maps, origins, shots):
    per_chunk = maps.shape[0] // chunks
    arrays, where = [], {}
    before = place

    def keep(value):
        arrays.append(value)
        return len(arrays) - 1

    for way in range(2):
        for g in range(grid.total):
            if grid.depth(way, g) == 0:
                dev, slot = grid.place(g)
                index = keep(origins[way][:, slot])
                for chunk in range(chunks):
                    where[way, chunk, g, dev] = index, chunk * per_chunk

    def fetch(holders):
        found = []
        for (index, part), devices in holders.items():
            array = arrays[index]
            if array.shape[0] != per_chunk:
                array = array[part : part + per_chunk]
            found.append((array, bits(devices)))
        return found[0][0] if len(found) == 1 else choose_step(found, place, groups)

    for kind, *body in program:
        if kind == "send":
            (messages,) = body
            chunk = messages[0][1]
            both = chunk < 0
            payloads, holders = [], []
            for c in range(chunks if both else 1):
                found = {}
                for way, chunk, value, here, there in messages:
                    found.setdefault(where[way, c if both else chunk, value, here], []).append(here)
                holders.append(found)
            if both and len(holders[0]) == 1 and len({i for found in holders for i, _ in found}) == 1:
                payload = arrays[next(iter(holders[0]))[0]]
            else:
                payloads = [fetch(found) for found in holders]
                payload = payloads[0] if len(payloads) == 1 else jnp.concatenate(payloads, axis=0)
            index = keep(lax.ppermute(payload, "sub", sorted((m[3], m[4]) for m in messages)))
            for way, chunk, value, _, there in messages:
                for c in range(chunks) if both else (chunk,):
                    where[way, c, value, there] = index, c * per_chunk if both else 0
            continue
        way, chunk, nodes = body
        steps, operands, made, count = [], [], {}, {}
        for value, dev in nodes:
            position = count.get(dev, 0)
            count[dev] = position + 1
            if position == len(steps):
                steps.append({"slot": {}, "arrays": {}, "earlier": {}, "sums": []})
            step = steps[position]
            g = value % grid.total
            step["slot"][dev] = grid.place(g)[1]
            inputs = grid.parents(way, g)
            if value >= grid.total:
                step["sums"].append(dev)
            elif (way, chunk, value + grid.total, dev) in where:
                inputs = [value + grid.total]
            for v in inputs:
                if (v, dev) in made:
                    earlier = made[v, dev]
                    step["earlier"][earlier] = step["earlier"].get(earlier, 0) | 1 << dev
                else:
                    index, part = where[way, chunk, v, dev]
                    if index not in operands:
                        operands.append(index)
                    index = operands.index(index), part
                    step["arrays"][index] = step["arrays"].get(index, 0) | 1 << dev
            made[value, dev] = position
        results = compute_step(
            way, range(chunk * per_chunk, (chunk + 1) * per_chunk), steps, place, groups, maps, origins[way],
            [arrays[i] for i in operands], before, shots
        )
        before = results[0]
        kept = [keep(r) for r in results]
        for (value, dev), position in made.items():
            where[way, chunk, value, dev] = kept[position], 0
    finished = {}
    for way in range(2):
        for chunk in range(chunks):
            for g in range(grid.total):
                dev, slot = grid.place(g)
                index, part = where[way, chunk, g, dev]
                for f in range(per_chunk):
                    places = finished.setdefault((way, chunk * per_chunk + f, slot), {})
                    places.setdefault((index, part + f), []).append(dev)
    return {key: [(arrays[i], f, bits(devs)) for (i, f), devs in found.items()] for key, found in finished.items()}


def interior_step(finished, place, maps, shots, groups, name):
    freqs, subs, _, width, _ = maps.shape
    one_slot = all(len({s for way, _, s in finished if way == w}) == 1 for w in range(2))
    slots = 1 if one_slot else subs
    columns = 2 * shots
    share = width // groups
    arrays, choices = [], {}
    for key, found in finished.items():
        choices[key] = []
        for array, f, mask in found:
            if not any(array is a for a in arrays):
                arrays.append(array)
            choices[key].append((next(i for i, a in enumerate(arrays) if a is array), f, mask))

    def kernel(place_ref, maps_ref, *refs):
        ins, (kept, back, sent), (both, wave) = refs[: len(arrays)], refs[len(arrays) : -2], refs[-2:]
        me, core = place_ref[0] // groups, lax.rem(place_ref[0], groups)
        for f in range(freqs):
            for s in range(subs):
                found = [(way, *c) for way in range(2) for c in choices.get((way, f, s), ())]
                if not found:
                    continue
                anyone = functools.reduce(lambda a, b: a | b, [c[-1] for c in found])

                @pl.when(flag(anyone, me))
                def _(f=f, s=s, found=found):
                    ways = sorted({c[0] for c in found})
                    for way, i, part, mask in found:

                        @pl.when(flag(mask, me))
                        def _(i=i, part=part, at=ways.index(way) * columns):
                            both[at : at + columns] = ins[i][part]

                    front = both[: len(ways) * columns]
                    by_real = lax.dot_general(front, maps_ref[f, s, 0], TIMES_TRANSPOSED, preferred_element_type=F32)
                    by_imag = lax.dot_general(front, maps_ref[f, s, 1], TIMES_TRANSPOSED, preferred_element_type=F32)
                    for at, way in enumerate(ways):
                        a, b = at * columns, at * columns + shots
                        real_part = (by_real[a : a + shots] - by_imag[b : b + shots]).astype(BF16)
                        imag_part = (by_real[b : b + shots] + by_imag[a : a + shots]).astype(BF16)
                        if way == 0:
                            wave[:shots] = real_part
                            wave[shots:] = imag_part
                            kept[f, s % slots] = wave[:, pl.ds(pl.multiple_of(core * share, share), share)]
                            for shift in range(1, groups):
                                owner = lax.rem(core + shift, groups)
                                rows = wave[:, pl.ds(pl.multiple_of(owner * share, share), share)]
                                sent[shift - 1, f, s % slots, :, :share] = rows
                        else:
                            back[f, s % slots, :shots] = real_part
                            back[f, s % slots, shots:] = imag_part
                            for shift in range(1, groups):
                                sent[shift - 1, f, s % slots, :shots, share:] = real_part
                                sent[shift - 1, f, s % slots, shots:, share:] = imag_part

    vmem = pl.BlockSpec(memory_space=pltpu.VMEM)
    return pl.pallas_call(
        kernel,
        out_shape=[
            jax.ShapeDtypeStruct((freqs, slots, columns, share), BF16),
            jax.ShapeDtypeStruct((freqs, slots, columns, width), BF16),
            jax.ShapeDtypeStruct((groups - 1, freqs, slots, columns, share + width), BF16),
        ],
        in_specs=[pl.BlockSpec(memory_space=pltpu.SMEM)] + [vmem] * (1 + len(arrays)),
        out_specs=[vmem] * 3,
        scratch_shapes=[pltpu.VMEM((2 * columns, width), BF16), pltpu.VMEM((columns, width), BF16)],
        compiler_params=pltpu.CompilerParams(vmem_limit_bytes=VMEM_LIMIT),
        cost_estimate=pl.CostEstimate(
            flops=8 * freqs * subs * columns * width * width, bytes_accessed=1 << 24, transcendentals=0
        ),
        name=name,
    )(place, maps, *arrays)


def exchange(sent, groups):
    received = []
    for shift in range(1, groups):
        ring = [(i, (i + shift) % groups) for i in range(groups)]
        received.append(lax.ppermute(sent[shift - 1], "freq", ring))
    return received


def image_step(early, late, late_masks, place, scale):
    kept, back, others = early
    freqs, subs, columns, share = kept.shape
    width = back.shape[-1]
    groups = 1 + len(others)
    total = groups * freqs * columns

    def kernel(place_ref, *refs):
        out, rows, points = refs[-3:]
        sets = [refs[: 1 + groups], refs[1 + groups : -3]]
        me = place_ref[0] // groups

        def copy(refs, s, way):
            s = s % refs[0].shape[1]
            for g in range(groups):
                for f in range(freqs):
                    at = pl.ds((g * freqs + f) * columns, columns)
                    if g == 0:
                        if way == 0:
                            rows[at] = refs[0][f, s]
                        else:
                            points[at] = refs[1][f, s]
                    elif way == 0:
                        rows[at] = refs[1 + g][f, s, :, :share]
                    else:
                        points[at] = refs[1 + g][f, s, :, share:]

        for s in range(subs):
            for way in range(2):
                mask = late_masks[way, s]
                if mask == 0:
                    copy(sets[0], s, way)
                else:
                    pl.when(jnp.logical_not(flag(mask, me)))(functools.partial(copy, sets[0], s, way))
                    pl.when(flag(mask, me))(functools.partial(copy, sets[1], s, way))
            out[s] = lax.dot_general(rows[...], points[...], TRANSPOSED_TIMES, preferred_element_type=F32) * scale

    vmem = pl.BlockSpec(memory_space=pltpu.VMEM)
    operands = [kept, back, *others]
    if late is not None:
        operands += [late[0], late[1], *late[2]]
    return pl.pallas_call(
        kernel,
        out_shape=jax.ShapeDtypeStruct((subs, share, width), F32),
        in_specs=[pl.BlockSpec(memory_space=pltpu.SMEM)] + [vmem] * len(operands),
        out_specs=vmem,
        scratch_shapes=[pltpu.VMEM((total, share), BF16), pltpu.VMEM((total, width), BF16)],
        compiler_params=pltpu.CompilerParams(vmem_limit_bytes=VMEM_LIMIT),
        name="image",
    )(place, *operands)


def choose_shots(shot_index, place, bank_size):
    def kernel(_, index_ref, out_ref):
        rows = lax.broadcasted_iota(jnp.int32, out_ref.shape, 0)
        out_ref[...] = (rows == index_ref[...]).astype(F32).astype(BF16)

    return pl.pallas_call(
        kernel,
        out_shape=jax.ShapeDtypeStruct((bank_size, shot_index.shape[0]), BF16),
        in_specs=[pl.BlockSpec(memory_space=pltpu.SMEM), pl.BlockSpec(memory_space=pltpu.VMEM)],
        out_specs=pl.BlockSpec(memory_space=pltpu.VMEM),
        name="shots",
    )(place, shot_index[None, :])


def pick_shots(table, chooser):
    freqs, subs, width, _, _ = table.shape
    picked = jnp.einsum("fsxcb,bn->fscnx", table, chooser, preferred_element_type=F32)
    return picked.astype(BF16).reshape(freqs, subs, -1, width)


def make_image(finished, last, place, maps, shots, groups, scale):
    subs = maps.shape[1]
    late_masks = {(way, s): bits([d for d, slot in last[way] if slot == s]) for way in range(2) for s in range(subs)}
    early_fronts, late_fronts = {}, {}
    for (way, f, s), found in finished.items():
        mask = late_masks[way, s]
        for array, part, devices in found:
            if devices & ~mask:
                early_fronts.setdefault((way, f, s), []).append((array, part, devices & ~mask))
            if devices & mask:
                late_fronts.setdefault((way, f, s), []).append((array, part, devices & mask))
    kept, back, sent = interior_step(early_fronts, place, maps, shots, groups, "interior")
    early = kept, back, exchange(sent, groups)
    late = None
    if late_fronts:
        kept, back, sent = interior_step(late_fronts, place, maps, shots, groups, "interior_last")
        late = kept, back, exchange(sent, groups)
    return image_step(early, late, late_masks, place, scale)


def per_device(trace_map, interior_map, excitation, receiver_data, shot_index):
    freq_local, sub_local = trace_map.shape[:2]
    shots = shot_index.shape[0]
    bank_size = excitation.shape[4]
    grid = Grid(sub_local * lax.axis_size("sub"), sub_local)
    groups = lax.axis_size("freq")
    place = (lax.axis_index("sub") * groups + lax.axis_index("freq")).astype(jnp.int32).reshape(1)
    chooser = choose_shots(shot_index, place, bank_size)
    origins = (pick_shots(excitation, chooser), pick_shots(receiver_data, chooser))
    scale = (2.0 * shots * freq_local * groups) ** (-0.5)
    deepest = grid.rows + GY - 2
    last = [[], []]
    if deepest <= TICKS:
        for way in range(2):
            last[way] = [grid.place(g) for g in range(grid.total) if grid.depth(way, g) == deepest]
        chunks, program = choose_program(grid, freq_local)
        finished = sweep(program, chunks, grid, place, groups, trace_map, origins, shots)
    else:
        finished = jacobi(grid, place // groups, trace_map, origins, shots)
    return make_image(finished, last, place, interior_map, shots, groups, scale)


def choose_program(grid, freqs):
    if (grid.rows, grid.devices, freqs % CHUNKS_OF_4X4) != (4, 8, 0):
        return 1, tick_program(grid, 1)
    kinds = ("send", "compute")
    return CHUNKS_OF_4X4, [(kinds[kind], *body) for kind, *body in PROGRAM_OF_4X4]


def jacobi(grid, device, maps, origins, shots):
    chunks, subs = maps.shape[:2]
    reach = GY // subs
    count = grid.devices
    places = (device[0] * subs + jnp.arange(subs, dtype=jnp.int32) + GY + 1) % grid.total
    column, row = places % GY, places // GY

    def move(x, by):
        return lax.ppermute(x, "sub", [(i, (i + by) % count) for i in range(count)])

    def mask(flags):
        return flags.astype(F32)[None, :, None, None]

    forward, adjoint = origins
    for _ in range(TICKS):
        left = jnp.concatenate([move(forward[:, subs - 1 :], 1), forward[:, : subs - 1]], axis=1)
        above = move(forward, reach)
        right = jnp.concatenate([adjoint[:, 1:], move(adjoint[:, :1], -1)], axis=1)
        below = move(adjoint, -reach)
        forward_in = left.astype(F32) * mask(column != 0) + above.astype(F32) * mask(row != 0)
        adjoint_in = right.astype(F32) * mask(column != GY - 1) + below.astype(F32) * mask(row != grid.rows - 1)
        fronts = []
        for way, total in enumerate((forward_in, adjoint_in)):
            dims = "fsnm,fsckm->fscnk" if way == 0 else "fsnk,fsckm->fscnm"
            product = jnp.einsum(dims, total.astype(BF16), maps, preferred_element_type=F32)
            real, imag = product[:, :, 0], product[:, :, 1]
            sign = 1.0 if way == 0 else -1.0
            moved = jnp.concatenate(
                [
                    real[:, :, :shots] - sign * imag[:, :, shots:],
                    real[:, :, shots:] + sign * imag[:, :, :shots],
                ],
                axis=2,
            )
            fronts.append((origins[way].astype(F32) + moved).astype(BF16))
        forward, adjoint = fronts
    everyone = bits(range(count))
    return {
        (way, f, s): [(front[:, s], f, everyone)]
        for way, front in enumerate((forward, adjoint))
        for f in range(chunks)
        for s in range(subs)
    }


def solution(mesh):
    placed = (
        P("freq", ("survey", "sub"), None, None, None),
        P("freq", ("survey", "sub"), None, None, None),
        P("freq", ("survey", "sub"), None, None, None),
        P("freq", ("survey", "sub"), None, None, None),
        P("survey"),
    )
    return jax.shard_map(
        per_device,
        mesh=mesh,
        in_specs=placed,
        out_specs=P(("survey", "sub"), "freq", None),
        check_vma=False,
    )
```

```python
import functools

import jax
import jax.numpy as jnp
import numpy as np
from jax import lax
from jax.experimental import pallas as pl
from jax.experimental.pallas import tpu as pltpu
from jax.sharding import PartitionSpec as P

GY = 4
TICKS = 6
BF16 = jnp.bfloat16
F32 = jnp.float32
TIMES = (((1,), (0,)), ((), ()))
TIMES_TRANSPOSED = (((1,), (1,)), ((), ()))
TRANSPOSED_TIMES = (((0,), (0,)), ((), ()))
VMEM_LIMIT = 12 * 1024 * 1024
CHUNKS_OF_4X4 = 1
PROGRAM_OF_4X4 = (
    (0, ((1, 0, 15, 5, 3),)),
    (0, ((1, 0, 15, 5, 4),)),
    (0, ((0, 0, 0, 5, 6),)),
    (1, 1, 0, ((11, 3),)),
    (0, ((1, 0, 11, 3, 2), (0, 0, 0, 5, 7))),
    (0, ((1, 0, 11, 3, 1),)),
    (1, 1, 0, ((14, 4),)),
    (0, ((1, 0, 14, 4, 2),)),
    (1, 1, 0, ((13, 4),)),
    (1, 0, 0, ((1, 6),)),
    (1, 0, 0, ((4, 7),)),
    (0, ((1, 0, 13, 4, 2), (0, 0, 4, 7, 1))),
    (1, 1, 0, ((7, 1),)),
    (0, ((1, 0, 7, 1, 0),)),
    (1, 1, 0, ((10, 2),)),
    (0, ((1, 0, 10, 2, 0),)),
    (0, ((1, 0, 7, 1, 7),)),
    (1, 0, 0, ((2, 6),)),
    (1, 1, 0, ((9, 2),)),
    (0, ((1, 0, 9, 2, 0),)),
    (0, ((1, 0, 13, 2, 3),)),
    (1, 1, 0, ((6, 0),)),
    (1, 0, 0, ((8, 1),)),
    (0, ((0, 0, 8, 1, 3),)),
    (0, ((0, 0, 4, 1, 0), (1, 0, 6, 0, 6), (0, 0, 2, 6, 7))),
    (1, 1, 0, ((3, 7),)),
    (0, ((0, 0, 1, 6, 0),)),
    (1, 1, 0, ((12, 3), (5, 0))),
    (0, ((0, 0, 2, 6, 0), (1, 0, 5, 0, 6), (1, 0, 12, 3, 1), (0, 0, 8, 1, 2))),
    (0, ((1, 0, 9, 0, 1),)),
    (1, 0, 0, ((12, 3),)),
    (1, 0, 0, ((5, 0),)),
    (0, ((0, 0, 5, 0, 2),)),
    (0, ((1, 0, 3, 7, 6),)),
    (1, 0, 0, ((3, 7),)),
    (1, 0, 0, ((6, 0),)),
    (0, ((0, 0, 3, 7, 1), (0, 0, 6, 0, 2))),
    (0, ((0, 0, 6, 0, 1),)),
    (1, 1, 0, ((8, 1),)),
    (0, ((1, 0, 8, 1, 7), (0, 0, 12, 3, 4))),
    (1, 0, 0, ((9, 2),)),
    (0, ((1, 0, 5, 6, 7), (0, 0, 9, 2, 4))),
    (1, 1, 0, ((2, 6),)),
    (1, 1, 0, ((1, 6),)),
    (1, 0, 0, ((10, 2),)),
    (0, ((0, 0, 10, 2, 4),)),
    (0, ((0, 0, 10, 2, 3),)),
    (1, 0, 0, ((7, 1),)),
    (0, ((0, 0, 7, 1, 3),)),
    (1, 1, 0, ((4, 7),)),
    (0, ((1, 0, 4, 7, 5),)),
    (0, ((1, 0, 1, 6, 5),)),
    (1, 0, 0, ((13, 4),)),
    (1, 0, 0, ((11, 3), (14, 4))),
    (0, ((0, 0, 11, 3, 5),)),
    (0, ((0, 0, 14, 4, 5),)),
    (1, 1, 0, ((0, 5),)),
    (1, 0, 0, ((15, 5),)),
)


class Grid:
    def __init__(self, total, sub_local):
        self.total, self.sub_local = total, sub_local
        self.devices, self.rows = total // sub_local, total // GY

    def place(self, g):
        s = (g - GY - 1) % self.total
        return s // self.sub_local, s % self.sub_local

    def parents(self, way, g):
        row, col = g // GY, g % GY
        if way == 0:
            return [g - 1] * (col != 0) + [g - GY] * (row != 0)
        return [g + 1] * (col != GY - 1) + [g + GY] * (row != self.rows - 1)

    def depth(self, way, g):
        row, col = g // GY, g % GY
        return row + col if way == 0 else self.rows - 1 - row + GY - 1 - col


def tick_program(grid, chunks):
    deepest = grid.rows + GY - 2
    program = []

    def sends(way, chunk, tick):
        permutes = []
        for g in range(grid.total):
            if grid.depth(way, g) != tick:
                continue
            here = grid.place(g)[0]
            for p in grid.parents(way, g):
                there = grid.place(p)[0]
                message = (way, chunk, p, there, here)
                if there == here or any(message in permute for permute in permutes):
                    continue
                for permute in permutes:
                    if all(m[3] != there and m[4] != here for m in permute):
                        permute.append(message)
                        break
                else:
                    permutes.append([message])
        program.extend(("send", permute) for permute in permutes)

    chains = [(way, chunk) for chunk in range(chunks) for way in range(2)]
    for way, chunk in chains:
        sends(way, chunk, 1)
    for tick in range(1, deepest + 1):
        for way, chunk in chains:
            nodes = [(g, grid.place(g)[0]) for g in range(grid.total) if grid.depth(way, g) == tick]
            program.append(("compute", way, chunk, nodes))
            sends(way, chunk, tick + 1)
    return program


def bits(devices):
    return sum(1 << d for d in devices)


def flag(mask, device):
    return ((mask >> device) & 1) == 1


def turn(front, shots):
    blocks = [front[at : at + shots] for at in range(0, front.shape[0], shots)]
    return jnp.concatenate([part for re, im in zip(blocks[::2], blocks[1::2]) for part in (-im, re)], axis=0)


def times_map(front, real_map, imag_map, shots):
    moved = lax.dot_general(real_map, front, TIMES_TRANSPOSED, preferred_element_type=F32)
    moved += lax.dot_general(imag_map, turn(front, shots), TIMES_TRANSPOSED, preferred_element_type=F32)
    return moved.T


def times_turned_map(front, real_map, imag_map, shots):
    by_real = lax.dot_general(front, real_map, TIMES, preferred_element_type=F32)
    return by_real + lax.dot_general(turn(front, shots), imag_map, TIMES, preferred_element_type=F32)


def times_adjoint(front, real_map, imag_map, shots):
    by_real = lax.dot_general(front, real_map, TIMES, preferred_element_type=F32)
    by_imag = lax.dot_general(turn(front, shots), imag_map, TIMES, preferred_element_type=F32)
    return by_real - by_imag


def transpose_step(maps):
    def kernel(maps_ref, out_ref):
        for f in range(maps.shape[0]):
            for s in range(maps.shape[1]):
                for c in range(maps.shape[2]):
                    out_ref[f, s, c] = maps_ref[f, s, c].T

    vmem = pl.BlockSpec(memory_space=pltpu.VMEM)
    return pl.pallas_call(
        kernel,
        out_shape=jax.ShapeDtypeStruct(maps.shape, BF16),
        in_specs=[vmem],
        out_specs=vmem,
        compiler_params=pltpu.CompilerParams(vmem_limit_bytes=2 * VMEM_LIMIT),
        name="transpose",
    )(maps)


def compute_step(way, chunk, steps, place, groups, maps, origin, arrays, before, shots):
    width = origin.shape[-1]
    shape = (len(chunk), 2 * shots, width)

    def kernel(place_ref, maps_ref, origin_ref, _, *refs):
        ins, outs, total = refs[: len(arrays)], refs[len(arrays) : -1], refs[-1]
        me = place_ref[0] // groups
        for out, step in zip(outs, steps):
            everyone = bits(step["slot"])

            @pl.when(flag(everyone, me))
            def _():
                sources = [(ins[i], part, mask) for (i, part), mask in step["arrays"].items()]
                sources += [(outs[i], 0, mask) for i, mask in step["earlier"].items()]
                if all(mask == everyone for _, _, mask in sources):
                    first, part, _ = sources[0]
                    front = first[pl.ds(part, len(chunk))]
                    if len(sources) > 1:
                        front = front.astype(F32)
                        for ref, part, _ in sources[1:]:
                            front += ref[pl.ds(part, len(chunk))].astype(F32)
                        front = front.astype(BF16)
                else:
                    total[...] = jnp.zeros_like(total)
                    for ref, part, mask in sources:

                        @pl.when(flag(mask, me))
                        def _(ref=ref, part=part):
                            total[...] += ref[pl.ds(part, len(chunk))].astype(F32)

                    front = total[...].astype(BF16)
                sums = step["sums"]
                if sums:

                    @pl.when(flag(bits(sums), me))
                    def _():
                        out[...] = front

                if len(sums) == len(step["slot"]):
                    return

                @pl.when(flag(everyone & ~bits(sums), me))
                def _():
                    slot = jnp.int32(0)
                    for s in range(1, origin_ref.shape[1]):
                        slot += s * ((bits([d for d, own in step["slot"].items() if own == s]) >> me) & 1)
                    for i, f in enumerate(chunk):
                        apply = times_adjoint if way else times_turned_map
                        moved = apply(front[i], maps_ref[f, slot, 0], maps_ref[f, slot, 1], shots)
                        out[i] = (origin_ref[f, slot].astype(F32) + moved).astype(BF16)

    vmem = pl.BlockSpec(memory_space=pltpu.VMEM)
    return pl.pallas_call(
        kernel,
        out_shape=[jax.ShapeDtypeStruct(shape, BF16)] * len(steps),
        in_specs=[pl.BlockSpec(memory_space=pltpu.SMEM), vmem, vmem, pl.BlockSpec(memory_space=pl.ANY)]
        + [vmem] * len(arrays),
        out_specs=[vmem] * len(steps),
        scratch_shapes=[pltpu.VMEM(shape, F32)],
        compiler_params=pltpu.CompilerParams(vmem_limit_bytes=VMEM_LIMIT),
        cost_estimate=pl.CostEstimate(flops=8 * shots * width * width, bytes_accessed=1 << 20, transcendentals=0),
        name=f"front_{way}_{chunk[0]}",
    )(place, maps, origin, before, *arrays)


def choose_step(found, place, groups):
    def kernel(place_ref, *refs):
        me = place_ref[0] // groups
        for ref, (_, mask) in zip(refs, found):

            @pl.when(flag(mask, me))
            def _(ref=ref):
                refs[-1][...] = ref[...]

    vmem = pl.BlockSpec(memory_space=pltpu.VMEM)
    return pl.pallas_call(
        kernel,
        out_shape=jax.ShapeDtypeStruct(found[0][0].shape, BF16),
        in_specs=[pl.BlockSpec(memory_space=pltpu.SMEM)] + [vmem] * len(found),
        out_specs=vmem,
        compiler_params=pltpu.CompilerParams(vmem_limit_bytes=VMEM_LIMIT),
        name="choose",
    )(place, *[array for array, _ in found])


def sweep(program, chunks, grid, place, groups, maps, origins, shots):
    per_chunk = maps.shape[0] // chunks
    arrays, where = [], {}
    done = 0
    before = place
    before = turned = transpose_step(maps)

    def keep(value):
        arrays.append(value)
        return len(arrays) - 1

    for way in range(2):
        for g in range(grid.total):
            if grid.depth(way, g) == 0:
                dev, slot = grid.place(g)
                index = keep(origins[way][:, slot])
                for chunk in range(chunks):
                    where[way, chunk, g, dev] = index, chunk * per_chunk

    def fetch(holders):
        found = []
        for (index, part), devices in holders.items():
            array = arrays[index]
            if array.shape[0] != per_chunk:
                array = array[part : part + per_chunk]
            found.append((array, bits(devices)))
        return found[0][0] if len(found) == 1 else choose_step(found, place, groups)

    for kind, *body in program:
        if kind == "send":
            (messages,) = body
            chunk = messages[0][1]
            both = chunk < 0
            payloads, holders = [], []
            for c in range(chunks if both else 1):
                found = {}
                for way, chunk, value, here, there in messages:
                    found.setdefault(where[way, c if both else chunk, value, here], []).append(here)
                holders.append(found)
            if both and len(holders[0]) == 1 and len({i for found in holders for i, _ in found}) == 1:
                payload = arrays[next(iter(holders[0]))[0]]
            else:
                payloads = [fetch(found) for found in holders]
                payload = payloads[0] if len(payloads) == 1 else jnp.concatenate(payloads, axis=0)
            index = keep(lax.ppermute(payload, "sub", sorted((m[3], m[4]) for m in messages)))
            for way, chunk, value, _, there in messages:
                for c in range(chunks) if both else (chunk,):
                    where[way, c, value, there] = index, c * per_chunk if both else 0
            continue
        way, chunk, nodes = body
        steps, operands, made, count = [], [], {}, {}
        for value, dev in nodes:
            position = count.get(dev, 0)
            count[dev] = position + 1
            if position == len(steps):
                steps.append({"slot": {}, "arrays": {}, "earlier": {}, "sums": []})
            step = steps[position]
            g = value % grid.total
            step["slot"][dev] = grid.place(g)[1]
            inputs = grid.parents(way, g)
            if value >= grid.total:
                step["sums"].append(dev)
            elif (way, chunk, value + grid.total, dev) in where:
                inputs = [value + grid.total]
            for v in inputs:
                if (v, dev) in made:
                    earlier = made[v, dev]
                    step["earlier"][earlier] = step["earlier"].get(earlier, 0) | 1 << dev
                else:
                    index, part = where[way, chunk, v, dev]
                    if index not in operands:
                        operands.append(index)
                    index = operands.index(index), part
                    step["arrays"][index] = step["arrays"].get(index, 0) | 1 << dev
            made[value, dev] = position
        results = compute_step(
            way, range(chunk * per_chunk, (chunk + 1) * per_chunk), steps, place, groups, maps if way else turned, origins[way],
            [arrays[i] for i in operands], before, shots
        )
        done += 1
        before = turned if done == 0 else results[0]
        kept = [keep(r) for r in results]
        for (value, dev), position in made.items():
            where[way, chunk, value, dev] = kept[position], 0
    finished = {}
    for way in range(2):
        for chunk in range(chunks):
            for g in range(grid.total):
                dev, slot = grid.place(g)
                index, part = where[way, chunk, g, dev]
                for f in range(per_chunk):
                    places = finished.setdefault((way, chunk * per_chunk + f, slot), {})
                    places.setdefault((index, part + f), []).append(dev)
    return {key: [(arrays[i], f, bits(devs)) for (i, f), devs in found.items()] for key, found in finished.items()}


def interior_step(finished, place, maps, shots, groups, name):
    freqs, subs, _, width, _ = maps.shape
    one_slot = all(len({s for way, _, s in finished if way == w}) == 1 for w in range(2))
    slots = 1 if one_slot else subs
    columns = 2 * shots
    share = width // groups
    arrays, choices = [], {}
    for key, found in finished.items():
        choices[key] = []
        for array, f, mask in found:
            if not any(array is a for a in arrays):
                arrays.append(array)
            choices[key].append((next(i for i, a in enumerate(arrays) if a is array), f, mask))

    def kernel(place_ref, maps_ref, *refs):
        ins, (kept, back, sent), (both, wave) = refs[: len(arrays)], refs[len(arrays) : -2], refs[-2:]
        me, core = place_ref[0] // groups, lax.rem(place_ref[0], groups)
        for f in range(freqs):
            for s in range(subs):
                found = [(way, *c) for way in range(2) for c in choices.get((way, f, s), ())]
                if not found:
                    continue
                anyone = functools.reduce(lambda a, b: a | b, [c[-1] for c in found])

                @pl.when(flag(anyone, me))
                def _(f=f, s=s, found=found):
                    ways = sorted({c[0] for c in found})
                    for way, i, part, mask in found:

                        @pl.when(flag(mask, me))
                        def _(i=i, part=part, at=ways.index(way) * columns):
                            both[at : at + columns] = ins[i][part]

                    front = both[: len(ways) * columns]
                    moved = times_map(front, maps_ref[f, s, 0], maps_ref[f, s, 1], shots).astype(BF16)
                    for at, way in enumerate(ways):
                        part = moved[at * columns : (at + 1) * columns]
                        if way == 0:
                            wave[...] = part
                            kept[f, s % slots] = wave[:, pl.ds(pl.multiple_of(core * share, share), share)]
                            for shift in range(1, groups):
                                owner = lax.rem(core + shift, groups)
                                rows = wave[:, pl.ds(pl.multiple_of(owner * share, share), share)]
                                sent[shift - 1, f, s % slots, :, :share] = rows
                        else:
                            back[f, s % slots] = part
                            for shift in range(1, groups):
                                sent[shift - 1, f, s % slots, :, share:] = part

    vmem = pl.BlockSpec(memory_space=pltpu.VMEM)
    return pl.pallas_call(
        kernel,
        out_shape=[
            jax.ShapeDtypeStruct((freqs, slots, columns, share), BF16),
            jax.ShapeDtypeStruct((freqs, slots, columns, width), BF16),
            jax.ShapeDtypeStruct((groups - 1, freqs, slots, columns, share + width), BF16),
        ],
        in_specs=[pl.BlockSpec(memory_space=pltpu.SMEM)] + [vmem] * (1 + len(arrays)),
        out_specs=[vmem] * 3,
        scratch_shapes=[pltpu.VMEM((2 * columns, width), BF16), pltpu.VMEM((columns, width), BF16)],
        compiler_params=pltpu.CompilerParams(vmem_limit_bytes=VMEM_LIMIT),
        cost_estimate=pl.CostEstimate(
            flops=8 * freqs * subs * columns * width * width, bytes_accessed=1 << 24, transcendentals=0
        ),
        name=name,
    )(place, maps, *arrays)


def exchange(sent, groups):
    received = []
    for shift in range(1, groups):
        ring = [(i, (i + shift) % groups) for i in range(groups)]
        received.append(lax.ppermute(sent[shift - 1], "freq", ring))
    return received


def image_step(early, late, late_masks, place, scale):
    kept, back, others = early
    freqs, subs, columns, share = kept.shape
    width = back.shape[-1]
    groups = 1 + len(others)
    total = groups * freqs * columns

    def kernel(place_ref, *refs):
        out, rows, points = refs[-3:]
        sets = [refs[: 1 + groups], refs[1 + groups : -3]]
        me = place_ref[0] // groups

        def copy(refs, s, way):
            s = s % refs[0].shape[1]
            for g in range(groups):
                for f in range(freqs):
                    at = pl.ds((g * freqs + f) * columns, columns)
                    if g == 0:
                        if way == 0:
                            rows[at] = refs[0][f, s]
                        else:
                            points[at] = refs[1][f, s]
                    elif way == 0:
                        rows[at] = refs[1 + g][f, s, :, :share]
                    else:
                        points[at] = refs[1 + g][f, s, :, share:]

        for s in range(subs):
            for way in range(2):
                mask = late_masks[way, s]
                if mask == 0:
                    copy(sets[0], s, way)
                else:
                    pl.when(jnp.logical_not(flag(mask, me)))(functools.partial(copy, sets[0], s, way))
                    pl.when(flag(mask, me))(functools.partial(copy, sets[1], s, way))
            out[s] = lax.dot_general(rows[...], points[...], TRANSPOSED_TIMES, preferred_element_type=F32) * scale

    vmem = pl.BlockSpec(memory_space=pltpu.VMEM)
    operands = [kept, back, *others]
    if late is not None:
        operands += [late[0], late[1], *late[2]]
    return pl.pallas_call(
        kernel,
        out_shape=jax.ShapeDtypeStruct((subs, share, width), F32),
        in_specs=[pl.BlockSpec(memory_space=pltpu.SMEM)] + [vmem] * len(operands),
        out_specs=vmem,
        scratch_shapes=[pltpu.VMEM((total, share), BF16), pltpu.VMEM((total, width), BF16)],
        compiler_params=pltpu.CompilerParams(vmem_limit_bytes=VMEM_LIMIT),
        name="image",
    )(place, *operands)


def choose_shots(shot_index, place, bank_size):
    def kernel(_, index_ref, out_ref):
        rows = lax.broadcasted_iota(jnp.int32, out_ref.shape, 0)
        out_ref[...] = (rows == index_ref[...]).astype(F32).astype(BF16)

    return pl.pallas_call(
        kernel,
        out_shape=jax.ShapeDtypeStruct((bank_size, shot_index.shape[0]), BF16),
        in_specs=[pl.BlockSpec(memory_space=pltpu.SMEM), pl.BlockSpec(memory_space=pltpu.VMEM)],
        out_specs=pl.BlockSpec(memory_space=pltpu.VMEM),
        name="shots",
    )(place, shot_index[None, :])


def pick_shots(table, chooser):
    freqs, subs, width, _, _ = table.shape
    picked = jnp.einsum("fsxcb,bn->fscnx", table, chooser, preferred_element_type=F32)
    return picked.astype(BF16).reshape(freqs, subs, -1, width)


def make_image(finished, last, place, maps, shots, groups, scale):
    subs = maps.shape[1]
    late_masks = {(way, s): bits([d for d, slot in last[way] if slot == s]) for way in range(2) for s in range(subs)}
    early_fronts, late_fronts = {}, {}
    for (way, f, s), found in finished.items():
        mask = late_masks[way, s]
        for array, part, devices in found:
            if devices & ~mask:
                early_fronts.setdefault((way, f, s), []).append((array, part, devices & ~mask))
            if devices & mask:
                late_fronts.setdefault((way, f, s), []).append((array, part, devices & mask))
    kept, back, sent = interior_step(early_fronts, place, maps, shots, groups, "interior")
    early = kept, back, exchange(sent, groups)
    late = None
    if late_fronts:
        kept, back, sent = interior_step(late_fronts, place, maps, shots, groups, "interior_last")
        late = kept, back, exchange(sent, groups)
    return image_step(early, late, late_masks, place, scale)


def per_device(trace_map, interior_map, excitation, receiver_data, shot_index):
    freq_local, sub_local = trace_map.shape[:2]
    shots = shot_index.shape[0]
    bank_size = excitation.shape[4]
    grid = Grid(sub_local * lax.axis_size("sub"), sub_local)
    groups = lax.axis_size("freq")
    place = (lax.axis_index("sub") * groups + lax.axis_index("freq")).astype(jnp.int32).reshape(1)
    chooser = choose_shots(shot_index, place, bank_size)
    origins = (pick_shots(excitation, chooser), pick_shots(receiver_data, chooser))
    scale = (2.0 * shots * freq_local * groups) ** (-0.5)
    deepest = grid.rows + GY - 2
    last = [[], []]
    if deepest <= TICKS:
        for way in range(2):
            last[way] = [grid.place(g) for g in range(grid.total) if grid.depth(way, g) == deepest]
        chunks, program = choose_program(grid, freq_local)
        finished = sweep(program, chunks, grid, place, groups, trace_map, origins, shots)
    else:
        finished = jacobi(grid, place // groups, trace_map, origins, shots)
    return make_image(finished, last, place, interior_map, shots, groups, scale)


def choose_program(grid, freqs):
    if (grid.rows, grid.devices, freqs % CHUNKS_OF_4X4) != (4, 8, 0):
        return 1, tick_program(grid, 1)
    kinds = ("send", "compute")
    return CHUNKS_OF_4X4, [(kinds[kind], *body) for kind, *body in PROGRAM_OF_4X4]


def jacobi(grid, device, maps, origins, shots):
    chunks, subs = maps.shape[:2]
    reach = GY // subs
    count = grid.devices
    places = (device[0] * subs + jnp.arange(subs, dtype=jnp.int32) + GY + 1) % grid.total
    column, row = places % GY, places // GY

    def move(x, by):
        return lax.ppermute(x, "sub", [(i, (i + by) % count) for i in range(count)])

    def mask(flags):
        return flags.astype(F32)[None, :, None, None]

    forward, adjoint = origins
    for _ in range(TICKS):
        left = jnp.concatenate([move(forward[:, subs - 1 :], 1), forward[:, : subs - 1]], axis=1)
        above = move(forward, reach)
        right = jnp.concatenate([adjoint[:, 1:], move(adjoint[:, :1], -1)], axis=1)
        below = move(adjoint, -reach)
        forward_in = left.astype(F32) * mask(column != 0) + above.astype(F32) * mask(row != 0)
        adjoint_in = right.astype(F32) * mask(column != GY - 1) + below.astype(F32) * mask(row != grid.rows - 1)
        fronts = []
        for way, total in enumerate((forward_in, adjoint_in)):
            dims = "fsnm,fsckm->fscnk" if way == 0 else "fsnk,fsckm->fscnm"
            product = jnp.einsum(dims, total.astype(BF16), maps, preferred_element_type=F32)
            real, imag = product[:, :, 0], product[:, :, 1]
            sign = 1.0 if way == 0 else -1.0
            moved = jnp.concatenate(
                [
                    real[:, :, :shots] - sign * imag[:, :, shots:],
                    real[:, :, shots:] + sign * imag[:, :, :shots],
                ],
                axis=2,
            )
            fronts.append((origins[way].astype(F32) + moved).astype(BF16))
        forward, adjoint = fronts
    everyone = bits(range(count))
    return {
        (way, f, s): [(front[:, s], f, everyone)]
        for way, front in enumerate((forward, adjoint))
        for f in range(chunks)
        for s in range(subs)
    }


def solution(mesh):
    placed = (
        P("freq", ("survey", "sub"), None, None, None),
        P("freq", ("survey", "sub"), None, None, None),
        P("freq", ("survey", "sub"), None, None, None),
        P("freq", ("survey", "sub"), None, None, None),
        P("survey"),
    )
    return jax.shard_map(
        per_device,
        mesh=mesh,
        in_specs=placed,
        out_specs=P(("survey", "sub"), "freq", None),
        check_vma=False,
    )
```

```python
import functools

import jax
import jax.numpy as jnp
import numpy as np
from jax import lax
from jax.experimental import pallas as pl
from jax.experimental.pallas import tpu as pltpu
from jax.sharding import PartitionSpec as P

GY = 4
TICKS = 6
BF16 = jnp.bfloat16
F32 = jnp.float32
TIMES = (((1,), (0,)), ((), ()))
TIMES_TRANSPOSED = (((1,), (1,)), ((), ()))
TRANSPOSED_TIMES = (((0,), (0,)), ((), ()))
VMEM_LIMIT = 12 * 1024 * 1024
CHUNKS_OF_4X4 = 1
PROGRAM_OF_4X4 = (
    (0, ((1, 0, 15, 5, 4),)),
    (0, ((1, 0, 15, 5, 3),)),
    (1, 1, 0, ((14, 4),)),
    (0, ((0, 0, 0, 5, 7), (1, 0, 14, 4, 2))),
    (1, 1, 0, ((13, 4),)),
    (1, 1, 0, ((11, 3),)),
    (0, ((1, 0, 11, 3, 1),)),
    (0, ((1, 0, 11, 3, 2),)),
    (1, 0, 0, ((4, 7),)),
    (0, ((1, 0, 13, 4, 2), (0, 0, 4, 7, 1))),
    (1, 1, 0, ((7, 1),)),
    (0, ((1, 0, 7, 1, 0),)),
    (1, 1, 0, ((10, 2),)),
    (0, ((1, 0, 10, 2, 0),)),
    (0, ((0, 0, 0, 5, 6),)),
    (0, ((1, 0, 7, 1, 7),)),
    (1, 1, 0, ((9, 2),)),
    (0, ((1, 0, 9, 2, 0),)),
    (1, 1, 0, ((6, 0),)),
    (0, ((0, 0, 4, 1, 0), (1, 0, 6, 0, 6), (1, 0, 13, 2, 3))),
    (1, 0, 0, ((1, 6), (2, 6))),
    (1, 0, 0, ((8, 1),)),
    (0, ((0, 0, 8, 1, 3),)),
    (1, 1, 0, ((3, 7),)),
    (0, ((0, 0, 1, 6, 0), (1, 0, 3, 7, 6))),
    (1, 1, 0, ((5, 0),)),
    (0, ((1, 0, 5, 0, 6), (0, 0, 2, 6, 7))),
    (0, ((0, 0, 2, 6, 0),)),
    (1, 1, 0, ((12, 3),)),
    (0, ((0, 0, 8, 1, 2), (1, 0, 12, 3, 1))),
    (1, 0, 0, ((12, 3),)),
    (1, 0, 0, ((5, 0),)),
    (0, ((0, 0, 5, 0, 2),)),
    (0, ((1, 0, 9, 0, 1),)),
    (1, 0, 0, ((3, 7),)),
    (1, 0, 0, ((6, 0),)),
    (0, ((0, 0, 3, 7, 1), (0, 0, 6, 0, 2))),
    (0, ((0, 0, 6, 0, 1), (0, 0, 12, 3, 4))),
    (1, 0, 0, ((9, 2),)),
    (0, ((1, 0, 5, 6, 7),)),
    (1, 1, 0, ((8, 1),)),
    (0, ((1, 0, 8, 1, 7), (0, 0, 9, 2, 4))),
    (1, 0, 0, ((10, 2),)),
    (0, ((0, 0, 10, 2, 4),)),
    (0, ((0, 0, 10, 2, 3),)),
    (1, 0, 0, ((7, 1),)),
    (0, ((0, 0, 7, 1, 3),)),
    (1, 1, 0, ((4, 7), (2, 6))),
    (0, ((1, 0, 4, 7, 5),)),
    (1, 1, 0, ((1, 6),)),
    (0, ((1, 0, 1, 6, 5),)),
    (1, 0, 0, ((13, 4),)),
    (1, 0, 0, ((14, 4),)),
    (0, ((0, 0, 14, 4, 5),)),
    (1, 0, 0, ((11, 3),)),
    (0, ((0, 0, 11, 3, 5),)),
    (1, 1, 0, ((0, 5),)),
    (1, 0, 0, ((15, 5),)),
)


class Grid:
    def __init__(self, total, sub_local):
        self.total, self.sub_local = total, sub_local
        self.devices, self.rows = total // sub_local, total // GY

    def place(self, g):
        s = (g - GY - 1) % self.total
        return s // self.sub_local, s % self.sub_local

    def parents(self, way, g):
        row, col = g // GY, g % GY
        if way == 0:
            return [g - 1] * (col != 0) + [g - GY] * (row != 0)
        return [g + 1] * (col != GY - 1) + [g + GY] * (row != self.rows - 1)

    def depth(self, way, g):
        row, col = g // GY, g % GY
        return row + col if way == 0 else self.rows - 1 - row + GY - 1 - col


def tick_program(grid, chunks):
    deepest = grid.rows + GY - 2
    program = []

    def sends(way, chunk, tick):
        permutes = []
        for g in range(grid.total):
            if grid.depth(way, g) != tick:
                continue
            here = grid.place(g)[0]
            for p in grid.parents(way, g):
                there = grid.place(p)[0]
                message = (way, chunk, p, there, here)
                if there == here or any(message in permute for permute in permutes):
                    continue
                for permute in permutes:
                    if all(m[3] != there and m[4] != here for m in permute):
                        permute.append(message)
                        break
                else:
                    permutes.append([message])
        program.extend(("send", permute) for permute in permutes)

    chains = [(way, chunk) for chunk in range(chunks) for way in range(2)]
    for way, chunk in chains:
        sends(way, chunk, 1)
    for tick in range(1, deepest + 1):
        for way, chunk in chains:
            nodes = [(g, grid.place(g)[0]) for g in range(grid.total) if grid.depth(way, g) == tick]
            program.append(("compute", way, chunk, nodes))
            sends(way, chunk, tick + 1)
    return program


def bits(devices):
    return sum(1 << d for d in devices)


def flag(mask, device):
    return ((mask >> device) & 1) == 1


def turn(front, shots):
    blocks = [front[at : at + shots] for at in range(0, front.shape[0], shots)]
    return jnp.concatenate([part for re, im in zip(blocks[::2], blocks[1::2]) for part in (-im, re)], axis=0)


def times_map(front, real_map, imag_map, shots):
    moved = lax.dot_general(real_map, front, TIMES_TRANSPOSED, preferred_element_type=F32)
    moved += lax.dot_general(imag_map, turn(front, shots), TIMES_TRANSPOSED, preferred_element_type=F32)
    return moved.T


def times_turned_map(front, real_map, imag_map, shots):
    by_real = lax.dot_general(front, real_map, TIMES, preferred_element_type=F32)
    return by_real + lax.dot_general(turn(front, shots), imag_map, TIMES, preferred_element_type=F32)


def times_adjoint(front, real_map, imag_map, shots):
    by_real = lax.dot_general(front, real_map, TIMES, preferred_element_type=F32)
    by_imag = lax.dot_general(turn(front, shots), imag_map, TIMES, preferred_element_type=F32)
    return by_real - by_imag


def transpose_step(maps):
    def kernel(maps_ref, out_ref):
        for f in range(maps.shape[0]):
            for s in range(maps.shape[1]):
                for c in range(maps.shape[2]):
                    out_ref[f, s, c] = maps_ref[f, s, c].T

    vmem = pl.BlockSpec(memory_space=pltpu.VMEM)
    return pl.pallas_call(
        kernel,
        out_shape=jax.ShapeDtypeStruct(maps.shape, BF16),
        in_specs=[vmem],
        out_specs=vmem,
        compiler_params=pltpu.CompilerParams(vmem_limit_bytes=2 * VMEM_LIMIT),
        name="transpose",
    )(maps)


def compute_step(way, chunk, steps, place, groups, maps, origin, arrays, before, shots):
    width = origin.shape[-1]
    shape = (len(chunk), 2 * shots, width)

    def kernel(place_ref, maps_ref, origin_ref, _, *refs):
        ins, outs, total = refs[: len(arrays)], refs[len(arrays) : -1], refs[-1]
        me = place_ref[0] // groups
        for out, step in zip(outs, steps):
            everyone = bits(step["slot"])

            @pl.when(flag(everyone, me))
            def _():
                sources = [(ins[i], part, mask) for (i, part), mask in step["arrays"].items()]
                sources += [(outs[i], 0, mask) for i, mask in step["earlier"].items()]
                if all(mask == everyone for _, _, mask in sources):
                    first, part, _ = sources[0]
                    front = first[pl.ds(part, len(chunk))]
                    if len(sources) > 1:
                        front = front.astype(F32)
                        for ref, part, _ in sources[1:]:
                            front += ref[pl.ds(part, len(chunk))].astype(F32)
                        front = front.astype(BF16)
                else:
                    total[...] = jnp.zeros_like(total)
                    for ref, part, mask in sources:

                        @pl.when(flag(mask, me))
                        def _(ref=ref, part=part):
                            total[...] += ref[pl.ds(part, len(chunk))].astype(F32)

                    front = total[...].astype(BF16)
                sums = step["sums"]
                if sums:

                    @pl.when(flag(bits(sums), me))
                    def _():
                        out[...] = front

                if len(sums) == len(step["slot"]):
                    return

                @pl.when(flag(everyone & ~bits(sums), me))
                def _():
                    slot = jnp.int32(0)
                    for s in range(1, origin_ref.shape[1]):
                        slot += s * ((bits([d for d, own in step["slot"].items() if own == s]) >> me) & 1)
                    for i, f in enumerate(chunk):
                        apply = times_adjoint if way else times_turned_map
                        moved = apply(front[i], maps_ref[f, slot, 0], maps_ref[f, slot, 1], shots)
                        out[i] = (origin_ref[f, slot].astype(F32) + moved).astype(BF16)

    vmem = pl.BlockSpec(memory_space=pltpu.VMEM)
    return pl.pallas_call(
        kernel,
        out_shape=[jax.ShapeDtypeStruct(shape, BF16)] * len(steps),
        in_specs=[pl.BlockSpec(memory_space=pltpu.SMEM), vmem, vmem, pl.BlockSpec(memory_space=pl.ANY)]
        + [vmem] * len(arrays),
        out_specs=[vmem] * len(steps),
        scratch_shapes=[pltpu.VMEM(shape, F32)],
        compiler_params=pltpu.CompilerParams(vmem_limit_bytes=VMEM_LIMIT),
        cost_estimate=pl.CostEstimate(flops=8 * shots * width * width, bytes_accessed=1 << 20, transcendentals=0),
        name=f"front_{way}_{chunk[0]}",
    )(place, maps, origin, before, *arrays)


def choose_step(found, place, groups):
    def kernel(place_ref, *refs):
        me = place_ref[0] // groups
        for ref, (_, mask) in zip(refs, found):

            @pl.when(flag(mask, me))
            def _(ref=ref):
                refs[-1][...] = ref[...]

    vmem = pl.BlockSpec(memory_space=pltpu.VMEM)
    return pl.pallas_call(
        kernel,
        out_shape=jax.ShapeDtypeStruct(found[0][0].shape, BF16),
        in_specs=[pl.BlockSpec(memory_space=pltpu.SMEM)] + [vmem] * len(found),
        out_specs=vmem,
        compiler_params=pltpu.CompilerParams(vmem_limit_bytes=VMEM_LIMIT),
        name="choose",
    )(place, *[array for array, _ in found])


def sweep(program, chunks, grid, place, groups, maps, origins, shots):
    per_chunk = maps.shape[0] // chunks
    arrays, where = [], {}
    done = 0
    before = place
    before = turned = transpose_step(maps)

    def keep(value):
        arrays.append(value)
        return len(arrays) - 1

    for way in range(2):
        for g in range(grid.total):
            if grid.depth(way, g) == 0:
                dev, slot = grid.place(g)
                index = keep(origins[way][:, slot])
                for chunk in range(chunks):
                    where[way, chunk, g, dev] = index, chunk * per_chunk

    def fetch(holders):
        found = []
        for (index, part), devices in holders.items():
            array = arrays[index]
            if array.shape[0] != per_chunk:
                array = array[part : part + per_chunk]
            found.append((array, bits(devices)))
        return found[0][0] if len(found) == 1 else choose_step(found, place, groups)

    for kind, *body in program:
        if kind == "send":
            (messages,) = body
            chunk = messages[0][1]
            both = chunk < 0
            payloads, holders = [], []
            for c in range(chunks if both else 1):
                found = {}
                for way, chunk, value, here, there in messages:
                    found.setdefault(where[way, c if both else chunk, value, here], []).append(here)
                holders.append(found)
            if both and len(holders[0]) == 1 and len({i for found in holders for i, _ in found}) == 1:
                payload = arrays[next(iter(holders[0]))[0]]
            else:
                payloads = [fetch(found) for found in holders]
                payload = payloads[0] if len(payloads) == 1 else jnp.concatenate(payloads, axis=0)
            index = keep(lax.ppermute(payload, "sub", sorted((m[3], m[4]) for m in messages)))
            for way, chunk, value, _, there in messages:
                for c in range(chunks) if both else (chunk,):
                    where[way, c, value, there] = index, c * per_chunk if both else 0
            continue
        way, chunk, nodes = body
        steps, operands, made, count = [], [], {}, {}
        for value, dev in nodes:
            position = count.get(dev, 0)
            count[dev] = position + 1
            if position == len(steps):
                steps.append({"slot": {}, "arrays": {}, "earlier": {}, "sums": []})
            step = steps[position]
            g = value % grid.total
            step["slot"][dev] = grid.place(g)[1]
            inputs = grid.parents(way, g)
            if value >= grid.total:
                step["sums"].append(dev)
            elif (way, chunk, value + grid.total, dev) in where:
                inputs = [value + grid.total]
            for v in inputs:
                if (v, dev) in made:
                    earlier = made[v, dev]
                    step["earlier"][earlier] = step["earlier"].get(earlier, 0) | 1 << dev
                else:
                    index, part = where[way, chunk, v, dev]
                    if index not in operands:
                        operands.append(index)
                    index = operands.index(index), part
                    step["arrays"][index] = step["arrays"].get(index, 0) | 1 << dev
            made[value, dev] = position
        results = compute_step(
            way, range(chunk * per_chunk, (chunk + 1) * per_chunk), steps, place, groups, maps if way else turned, origins[way],
            [arrays[i] for i in operands], before, shots
        )
        done += 1
        before = turned if done == 0 else results[0]
        kept = [keep(r) for r in results]
        for (value, dev), position in made.items():
            where[way, chunk, value, dev] = kept[position], 0
    finished = {}
    for way in range(2):
        for chunk in range(chunks):
            for g in range(grid.total):
                dev, slot = grid.place(g)
                index, part = where[way, chunk, g, dev]
                for f in range(per_chunk):
                    places = finished.setdefault((way, chunk * per_chunk + f, slot), {})
                    places.setdefault((index, part + f), []).append(dev)
    return {key: [(arrays[i], f, bits(devs)) for (i, f), devs in found.items()] for key, found in finished.items()}


def interior_step(finished, place, maps, shots, groups, name):
    freqs, subs, _, width, _ = maps.shape
    one_slot = all(len({s for way, _, s in finished if way == w}) == 1 for w in range(2))
    slots = 1 if one_slot else subs
    columns = 2 * shots
    share = width // groups
    arrays, choices = [], {}
    for key, found in finished.items():
        choices[key] = []
        for array, f, mask in found:
            if not any(array is a for a in arrays):
                arrays.append(array)
            choices[key].append((next(i for i, a in enumerate(arrays) if a is array), f, mask))

    def kernel(place_ref, maps_ref, *refs):
        ins, (kept, back, sent), (both, wave) = refs[: len(arrays)], refs[len(arrays) : -2], refs[-2:]
        me, core = place_ref[0] // groups, lax.rem(place_ref[0], groups)
        for f in range(freqs):
            for s in range(subs):
                found = [(way, *c) for way in range(2) for c in choices.get((way, f, s), ())]
                if not found:
                    continue
                anyone = functools.reduce(lambda a, b: a | b, [c[-1] for c in found])

                @pl.when(flag(anyone, me))
                def _(f=f, s=s, found=found):
                    ways = sorted({c[0] for c in found})
                    for way, i, part, mask in found:

                        @pl.when(flag(mask, me))
                        def _(i=i, part=part, at=ways.index(way) * columns):
                            both[at : at + columns] = ins[i][part]

                    front = both[: len(ways) * columns]
                    moved = times_map(front, maps_ref[f, s, 0], maps_ref[f, s, 1], shots).astype(BF16)
                    for at, way in enumerate(ways):
                        part = moved[at * columns : (at + 1) * columns]
                        if way == 0:
                            wave[...] = part
                            kept[f, s % slots] = wave[:, pl.ds(pl.multiple_of(core * share, share), share)]
                            for shift in range(1, groups):
                                owner = lax.rem(core + shift, groups)
                                rows = wave[:, pl.ds(pl.multiple_of(owner * share, share), share)]
                                sent[shift - 1, f, s % slots, :, :share] = rows
                        else:
                            back[f, s % slots] = part
                            for shift in range(1, groups):
                                sent[shift - 1, f, s % slots, :, share:] = part

    vmem = pl.BlockSpec(memory_space=pltpu.VMEM)
    return pl.pallas_call(
        kernel,
        out_shape=[
            jax.ShapeDtypeStruct((freqs, slots, columns, share), BF16),
            jax.ShapeDtypeStruct((freqs, slots, columns, width), BF16),
            jax.ShapeDtypeStruct((groups - 1, freqs, slots, columns, share + width), BF16),
        ],
        in_specs=[pl.BlockSpec(memory_space=pltpu.SMEM)] + [vmem] * (1 + len(arrays)),
        out_specs=[vmem] * 3,
        scratch_shapes=[pltpu.VMEM((2 * columns, width), BF16), pltpu.VMEM((columns, width), BF16)],
        compiler_params=pltpu.CompilerParams(vmem_limit_bytes=VMEM_LIMIT),
        cost_estimate=pl.CostEstimate(
            flops=8 * freqs * subs * columns * width * width, bytes_accessed=1 << 24, transcendentals=0
        ),
        name=name,
    )(place, maps, *arrays)


def exchange(sent, groups):
    received = []
    for shift in range(1, groups):
        ring = [(i, (i + shift) % groups) for i in range(groups)]
        received.append(lax.ppermute(sent[shift - 1], "freq", ring))
    return received


def image_step(early, late, late_masks, place, scale):
    kept, back, others = early
    freqs, subs, columns, share = kept.shape
    width = back.shape[-1]
    groups = 1 + len(others)
    total = groups * freqs * columns

    def kernel(place_ref, *refs):
        out, rows, points = refs[-3:]
        sets = [refs[: 1 + groups], refs[1 + groups : -3]]
        me = place_ref[0] // groups

        def copy(refs, s, way):
            s = s % refs[0].shape[1]
            for g in range(groups):
                for f in range(freqs):
                    at = pl.ds((g * freqs + f) * columns, columns)
                    if g == 0:
                        if way == 0:
                            rows[at] = refs[0][f, s]
                        else:
                            points[at] = refs[1][f, s]
                    elif way == 0:
                        rows[at] = refs[1 + g][f, s, :, :share]
                    else:
                        points[at] = refs[1 + g][f, s, :, share:]

        for s in range(subs):
            for way in range(2):
                mask = late_masks[way, s]
                if mask == 0:
                    copy(sets[0], s, way)
                else:
                    pl.when(jnp.logical_not(flag(mask, me)))(functools.partial(copy, sets[0], s, way))
                    pl.when(flag(mask, me))(functools.partial(copy, sets[1], s, way))
            out[s] = lax.dot_general(rows[...], points[...], TRANSPOSED_TIMES, preferred_element_type=F32) * scale

    vmem = pl.BlockSpec(memory_space=pltpu.VMEM)
    operands = [kept, back, *others]
    if late is not None:
        operands += [late[0], late[1], *late[2]]
    return pl.pallas_call(
        kernel,
        out_shape=jax.ShapeDtypeStruct((subs, share, width), F32),
        in_specs=[pl.BlockSpec(memory_space=pltpu.SMEM)] + [vmem] * len(operands),
        out_specs=vmem,
        scratch_shapes=[pltpu.VMEM((total, share), BF16), pltpu.VMEM((total, width), BF16)],
        compiler_params=pltpu.CompilerParams(vmem_limit_bytes=VMEM_LIMIT),
        name="image",
    )(place, *operands)


def choose_shots(shot_index, place, bank_size):
    def kernel(_, index_ref, out_ref):
        rows = lax.broadcasted_iota(jnp.int32, out_ref.shape, 0)
        out_ref[...] = (rows == index_ref[...]).astype(F32).astype(BF16)

    return pl.pallas_call(
        kernel,
        out_shape=jax.ShapeDtypeStruct((bank_size, shot_index.shape[0]), BF16),
        in_specs=[pl.BlockSpec(memory_space=pltpu.SMEM), pl.BlockSpec(memory_space=pltpu.VMEM)],
        out_specs=pl.BlockSpec(memory_space=pltpu.VMEM),
        name="shots",
    )(place, shot_index[None, :])


def pick_shots(table, chooser):
    freqs, subs, width, _, _ = table.shape
    picked = jnp.einsum("fsxcb,bn->fscnx", table, chooser, preferred_element_type=F32)
    return picked.astype(BF16).reshape(freqs, subs, -1, width)


def make_image(finished, last, place, maps, shots, groups, scale):
    subs = maps.shape[1]
    late_masks = {(way, s): bits([d for d, slot in last[way] if slot == s]) for way in range(2) for s in range(subs)}
    early_fronts, late_fronts = {}, {}
    for (way, f, s), found in finished.items():
        mask = late_masks[way, s]
        for array, part, devices in found:
            if devices & ~mask:
                early_fronts.setdefault((way, f, s), []).append((array, part, devices & ~mask))
            if devices & mask:
                late_fronts.setdefault((way, f, s), []).append((array, part, devices & mask))
    kept, back, sent = interior_step(early_fronts, place, maps, shots, groups, "interior")
    early = kept, back, exchange(sent, groups)
    late = None
    if late_fronts:
        kept, back, sent = interior_step(late_fronts, place, maps, shots, groups, "interior_last")
        late = kept, back, exchange(sent, groups)
    return image_step(early, late, late_masks, place, scale)


def per_device(trace_map, interior_map, excitation, receiver_data, shot_index):
    freq_local, sub_local = trace_map.shape[:2]
    shots = shot_index.shape[0]
    bank_size = excitation.shape[4]
    grid = Grid(sub_local * lax.axis_size("sub"), sub_local)
    groups = lax.axis_size("freq")
    place = (lax.axis_index("sub") * groups + lax.axis_index("freq")).astype(jnp.int32).reshape(1)
    chooser = choose_shots(shot_index, place, bank_size)
    origins = (pick_shots(excitation, chooser), pick_shots(receiver_data, chooser))
    scale = (2.0 * shots * freq_local * groups) ** (-0.5)
    deepest = grid.rows + GY - 2
    last = [[], []]
    if deepest <= TICKS:
        for way in range(2):
            last[way] = [grid.place(g) for g in range(grid.total) if grid.depth(way, g) == deepest]
        chunks, program = choose_program(grid, freq_local)
        finished = sweep(program, chunks, grid, place, groups, trace_map, origins, shots)
    else:
        finished = jacobi(grid, place // groups, trace_map, origins, shots)
    return make_image(finished, last, place, interior_map, shots, groups, scale)


def choose_program(grid, freqs):
    if (grid.rows, grid.devices, freqs % CHUNKS_OF_4X4) != (4, 8, 0):
        return 1, tick_program(grid, 1)
    kinds = ("send", "compute")
    return CHUNKS_OF_4X4, [(kinds[kind], *body) for kind, *body in PROGRAM_OF_4X4]


def jacobi(grid, device, maps, origins, shots):
    chunks, subs = maps.shape[:2]
    reach = GY // subs
    count = grid.devices
    places = (device[0] * subs + jnp.arange(subs, dtype=jnp.int32) + GY + 1) % grid.total
    column, row = places % GY, places // GY

    def move(x, by):
        return lax.ppermute(x, "sub", [(i, (i + by) % count) for i in range(count)])

    def mask(flags):
        return flags.astype(F32)[None, :, None, None]

    forward, adjoint = origins
    for _ in range(TICKS):
        left = jnp.concatenate([move(forward[:, subs - 1 :], 1), forward[:, : subs - 1]], axis=1)
        above = move(forward, reach)
        right = jnp.concatenate([adjoint[:, 1:], move(adjoint[:, :1], -1)], axis=1)
        below = move(adjoint, -reach)
        forward_in = left.astype(F32) * mask(column != 0) + above.astype(F32) * mask(row != 0)
        adjoint_in = right.astype(F32) * mask(column != GY - 1) + below.astype(F32) * mask(row != grid.rows - 1)
        fronts = []
        for way, total in enumerate((forward_in, adjoint_in)):
            dims = "fsnm,fsckm->fscnk" if way == 0 else "fsnk,fsckm->fscnm"
            product = jnp.einsum(dims, total.astype(BF16), maps, preferred_element_type=F32)
            real, imag = product[:, :, 0], product[:, :, 1]
            sign = 1.0 if way == 0 else -1.0
            moved = jnp.concatenate(
                [
                    real[:, :, :shots] - sign * imag[:, :, shots:],
                    real[:, :, shots:] + sign * imag[:, :, :shots],
                ],
                axis=2,
            )
            fronts.append((origins[way].astype(F32) + moved).astype(BF16))
        forward, adjoint = fronts
    everyone = bits(range(count))
    return {
        (way, f, s): [(front[:, s], f, everyone)]
        for way, front in enumerate((forward, adjoint))
        for f in range(chunks)
        for s in range(subs)
    }


def solution(mesh):
    placed = (
        P("freq", ("survey", "sub"), None, None, None),
        P("freq", ("survey", "sub"), None, None, None),
        P("freq", ("survey", "sub"), None, None, None),
        P("freq", ("survey", "sub"), None, None, None),
        P("survey"),
    )
    return jax.shard_map(
        per_device,
        mesh=mesh,
        in_specs=placed,
        out_specs=P(("survey", "sub"), "freq", None),
        check_vma=False,
    )
```
